32 devices in a mesh: ens: 2 (over y), ty: 4 (over z), tx: 4 (over x, core).
Axes of the slice: x: 2, y: 2, z: 4, core: 2. Of those that a mesh axis runs over, the one named last changes fastest.
Arguments:
- perturbations: bfloat16 [32, 3, 512, 512], P('ens', None, 'ty', 'tx'), may hold values from -1 to 1
- ens_weights: float32 [32, 512, 512], P('ens', 'ty', 'tx'), may hold values from -6 to 6
- control: float32 [3, 512, 512], P(None, 'ty', 'tx'), may hold values from -6 to 6
- static_std: float32 [3, 512, 512], P(None, 'ty', 'tx'), may hold values from 0.2 to 1
- courant: float32 [512, 512], P('ty', 'tx'), may hold values from 0.05 to 0.4
- land_mask: int32 [512, 512], P('ty', 'tx'), may hold values 0 or 1
- band_offsets: int32 [32], replicated, may hold values from 0 to 31
- band_weights: float32 [32], replicated, may hold values from 0.05 to 1
- obs_cells: int32 [4, 4, 6, 512], P('ty', 'tx'), may hold values from 0 to 16383
- obs_values: float32 [4, 4, 6, 512], P('ty', 'tx'), may hold values from -4 to 4
- obs_weights: float32 [4, 4, 6, 512], P('ty', 'tx'), may hold values from 0.5 to 2
Outputs:
- control_new: float32 [3, 512, 512], P(None, 'ty', 'tx')
- weights_new: float32 [32, 512, 512], P('ens', 'ty', 'tx')
- cost_value: float32 [], replicated
The draws below stay inside these ranges and needn't reach their ends.
Inputs may be any that keep to these rules, and one draw needn't show every extreme that they name: `obs_cells`: row-major index of a cell within the observing tile of 128 x 128 cells.
All inputs are finite; a program needn't handle non-finite values. No bound on the sum of `land_mask` on one device may be relied on, other than what follows from the above.
Results may differ from the reference program's by a relative error of at most 0.0003.
Values may be sent and summed in bfloat16 or wider, within the bound.
No kernel may reach another device: no remote copies, remote signals or barrier semaphores. Data moves between devices by JAX's collectives and lax.ppermute only.
A program may use at most 128 MiB of HBM per device.

```python
import math
import jax
import jax.numpy as jnp
from jax import lax

M_DEV = 16
CY = 128
CX = 128
STEPS = 6
OBS = 512
MEMBERS = 32
NY = 512
NX = 512
N_TY = 4
N_TX = 4


def plant(entries, rng, least, top_value):
    shape = entries.shape
    index_at = [jax.random.randint(jax.random.fold_in(rng, axis), (), 0, shape[axis]) for axis in range(len(shape))]
    entries = entries.at[tuple(index_at)].set(least)
    longest = shape.index(max(shape))
    index_at[longest] = (index_at[longest] + 1) % shape[longest]
    return entries.at[tuple(index_at)].set(top_value)


def level_of(stream_key, extent, pieces, low, top_value):
    def one(position, shards_of):
        steps = jax.random.uniform(jax.random.fold_in(jax.random.fold_in(stream_key, 6), position), (shards_of,), jnp.float32, low / len(pieces), top_value / len(pieces))
        return jnp.repeat(jnp.exp(steps), extent[position] // shards_of).reshape((-1,) + (1,) * (len(extent) - position - 1))

    level = one(*pieces[0])
    for cut in pieces[1:]:
        level = level * one(*cut)
    return level


def gaussian(stream_key, dims, width, most, cuts=(), held_as=jnp.bfloat16):
    loudness = level_of(stream_key, dims, cuts, -0.22, 0.18) if cuts else 1.0
    entries = jax.random.normal(stream_key, dims, jnp.float32) * width * loudness
    return jnp.minimum(jnp.maximum(entries, -most), most).astype(held_as)


def setup_inputs(seed: int = 0) -> dict:
    splits = jax.random.split(jax.random.key(seed), 12)
    return {
        "perturbations": gaussian(splits[0], (MEMBERS, 3, NY, NX), MEMBERS ** -0.5, 1.0, ((0, 2), (2, 4), (3, 4))),
        "ens_weights": gaussian(splits[1], (MEMBERS, NY, NX), 1.0, 6.0, ((0, 2), (1, 4), (2, 4)), jnp.float32),
        "control": gaussian(splits[2], (3, NY, NX), 1.0, 6.0, ((1, 4), (2, 4)), jnp.float32),
        "static_std": jnp.clip(jnp.exp(math.log(1.0) - 1.609438 * jax.random.uniform(splits[3], (3, NY, NX), jnp.float32) ** level_of(splits[3], (3, NY, NX), ((1, 4), (2, 4)), -0.2, 0.2)), 0.2, 1.0),
        "courant": jnp.clip(jnp.exp(math.log(0.4) - 2.0794415 * jax.random.uniform(splits[4], (NY, NX), jnp.float32) ** level_of(splits[4], (NY, NX), ((0, 4), (1, 4)), -0.2, 0.2)), 0.05, 0.4),
        "land_mask": plant((jax.random.randint(splits[5], (NY, NX), 0, 5) < 4).astype(jnp.int32), jax.random.fold_in(splits[5], 1), 0, 1),
        "band_offsets": plant(jax.random.randint(splits[6], (MEMBERS,), 0, MEMBERS), jax.random.fold_in(splits[6], 1), 0, MEMBERS - 1).astype(jnp.int32),
        "band_weights": jnp.clip(jnp.exp(jax.random.uniform(splits[7], (MEMBERS,), jnp.float32, math.log(0.05), math.log(1.0))), 0.05, 1.0),
        "obs_cells": plant(jax.random.randint(splits[8], (N_TY, N_TX, STEPS, OBS), 0, CY * CX), jax.random.fold_in(splits[8], 1), 0, (CY * CX) - 1).astype(jnp.int32),
        "obs_values": gaussian(splits[9], (N_TY, N_TX, STEPS, OBS), 0.5, 4.0, ((0, 4), (1, 4)), jnp.float32),
        "obs_weights": jnp.clip(jnp.exp(math.log(2.0) - 1.3862944 * jax.random.uniform(splits[10], (N_TY, N_TX, STEPS, OBS), jnp.float32) ** level_of(splits[10], (N_TY, N_TX, STEPS, OBS), ((0, 4), (1, 4)), -0.2, 0.2)), 0.5, 2.0),
    }


step_length = 0.25

def band_matrix(band_offsets, band_weights):
    member_count = band_weights.shape[0]
    doubled = jnp.concatenate([band_weights, band_weights])

    def one_row(offset):
        return lax.dynamic_slice_in_dim(doubled, (member_count - offset).astype(jnp.int32), member_count)
    return jax.vmap(one_row)(band_offsets).astype(jnp.bfloat16)

def diff_x(field):
    return 0.5 * (jnp.roll(field, -1, -1) - jnp.roll(field, 1, -1))

def diff_y(field):
    padded = jnp.pad(field, ((1, 1), (0, 0)))
    return 0.5 * (padded[2:] - padded[:-2])

def advance(height, east_vel, north_vel, wet_mask, courant):
    east_new = wet_mask * (east_vel - diff_x(height))
    north_new = wet_mask * (north_vel - diff_y(height))
    height_new = height - diff_x(courant * east_new) - diff_y(courant * north_new)
    return (height_new, east_new, north_new)

def retreat(adj_height, adj_east, adj_north, wet_mask, courant):
    east_sum = wet_mask * (adj_east + courant * diff_x(adj_height))
    north_sum = wet_mask * (adj_north + courant * diff_y(adj_height))
    return (adj_height + diff_x(east_sum) + diff_y(north_sum), east_sum, north_sum)

def reference(perturbations, ens_weights, control, static_std, courant, land_mask, band_offsets, band_weights, obs_cells, obs_values, obs_weights):
    tile_cells = NY * NX
    ens_scale = 1.0 / math.sqrt(MEMBERS)
    band = band_matrix(band_offsets, band_weights)
    flat = perturbations.reshape(MEMBERS, 3 * tile_cells)
    block_count = MEMBERS // M_DEV

    def block_modes(index):
        rows_band = lax.dynamic_slice_in_dim(band, (index * M_DEV).astype(jnp.int32), M_DEV, 0)
        return jnp.dot(rows_band, flat, preferred_element_type=jnp.float32).reshape(M_DEV, 3, NY, NX)

    def block_weights(index):
        return lax.dynamic_slice_in_dim(ens_weights, (index * M_DEV).astype(jnp.int32), M_DEV, 0)

    def add_block(total, index):
        modes = block_modes(index)
        return (total + lax.optimization_barrier(jnp.sum(block_weights(index)[:, None] * modes, axis=0)), None)
    ens_part, _ = lax.scan(add_block, jnp.zeros((3, NY, NX), jnp.float32), jnp.arange(block_count).astype(jnp.int32))
    increment = static_std * control + ens_scale * ens_part
    wet_mask = land_mask.astype(jnp.float32)
    tile_row = (jnp.arange(N_TY) * CY).astype(jnp.int32)[:, None, None, None]
    tile_col = (jnp.arange(N_TX) * CX).astype(jnp.int32)[None, :, None, None]
    glob_row = tile_row + obs_cells // CX
    glob_col = tile_col + obs_cells % CX
    height, east_vel, north_vel = (increment[0], increment[1], increment[2])
    weighted_list = []
    misfit_sum = jnp.zeros((), jnp.float32)
    for step in range(STEPS):
        height, east_vel, north_vel = advance(height, east_vel, north_vel, wet_mask, courant)
        seen = height[glob_row[:, :, step], glob_col[:, :, step]]
        misfit = seen - obs_values[:, :, step]
        weighted = obs_weights[:, :, step] * misfit
        weighted_list.append(weighted)
        misfit_sum = misfit_sum + jnp.sum(weighted * misfit)
    adj_height = jnp.zeros((NY, NX), jnp.float32)
    adj_east = jnp.zeros((NY, NX), jnp.float32)
    adj_north = jnp.zeros((NY, NX), jnp.float32)
    for step in range(STEPS - 1, -1, -1):
        adj_height = adj_height.at[glob_row[:, :, step], glob_col[:, :, step]].add(weighted_list[step])
        adj_height, adj_east, adj_north = retreat(adj_height, adj_east, adj_north, wet_mask, courant)
    lam_zero = jnp.stack([adj_height, adj_east, adj_north])
    control_new = control - step_length * (control + static_std * lam_zero)

    def new_block(index):
        modes = block_modes(index)
        alphas = block_weights(index)
        grad = alphas + ens_scale * lax.optimization_barrier(jnp.sum(modes * lam_zero[None], axis=1))
        return alphas - step_length * grad
    weights_new = lax.map(new_block, jnp.arange(block_count).astype(jnp.int32)).reshape(MEMBERS, NY, NX)
    total = jnp.sum(control * control) + jnp.sum(ens_weights * ens_weights) + misfit_sum
    cost_value = 0.5 * total / ((3 + MEMBERS) * tile_cells)
    return (control_new, weights_new, cost_value)
```

```python
import functools
import math

import jax
import jax.numpy as jnp
from jax import lax
from jax.experimental import pallas as pl
from jax.experimental.pallas import tpu as pltpu
from jax.sharding import PartitionSpec as P

step_length = 0.25
SUB = 16
F32 = jnp.float32
BF16 = jnp.bfloat16
VMEM = pl.BlockSpec(memory_space=pltpu.VMEM)
SMEM = pl.BlockSpec(memory_space=pltpu.SMEM)


def call(kernel, outs, ins, scratch=(), smem=0, flops=0, name=None):
    out_shape = [jax.ShapeDtypeStruct(s, d) for s, d in outs]
    moved = sum(math.prod(s) * jnp.dtype(d).itemsize for s, d in outs)
    moved += sum(x.size * x.dtype.itemsize for x in ins)
    return pl.pallas_call(
        kernel,
        out_shape=out_shape,
        in_specs=[SMEM] * smem + [VMEM] * (len(ins) - smem),
        out_specs=[VMEM] * len(outs),
        scratch_shapes=list(scratch),
        compiler_params=pltpu.CompilerParams(vmem_limit_bytes=40 * 1024 * 1024),
        cost_estimate=pl.CostEstimate(flops=flops, bytes_accessed=moved, transcendentals=0),
        name=name,
    )(*ins)


def split(x):
    hi = x.astype(BF16)
    return hi, (x - hi.astype(F32)).astype(BF16)


def folded(x):
    cols = x.shape[-1]
    return jnp.sum(x.reshape(-1, 8, cols), axis=0)


def maps_kernel(steps, cells_ref, values_ref, weights_ref, control_ref, maps_ref, cost_ref):
    rows, cols = maps_ref.shape[1:]
    count = cells_ref.shape[1]
    shift = cols.bit_length() - 1
    row_iota = lax.broadcasted_iota(jnp.int32, (rows, count), 0)
    col_iota = lax.broadcasted_iota(jnp.int32, (cols, count), 0)
    for t in range(steps):
        cells = cells_ref[t : t + 1, :]
        weight = weights_ref[t : t + 1, :]
        product = weight * values_ref[t : t + 1, :]
        at_row = jnp.where(row_iota == (cells >> shift), 1.0, 0.0).astype(BF16)
        hit = col_iota == (cells & (cols - 1))
        parts = []
        for value in (weight, product):
            for piece in split(value):
                parts.append(jnp.where(hit, piece.astype(F32), 0.0).astype(BF16))
        sums = lax.dot_general(
            at_row,
            jnp.concatenate(parts, axis=0),
            (((1,), (1,)), ((), ())),
            preferred_element_type=F32,
        )
        maps_ref[t] = sums[:, :cols] + sums[:, cols : 2 * cols]
        maps_ref[steps + t] = sums[:, 2 * cols : 3 * cols] + sums[:, 3 * cols :]
    value = values_ref[...]
    fixed = jnp.sum(weights_ref[...] * value * value, axis=0, keepdims=True)
    line = sum(fixed[:, k : k + cols] for k in range(0, count, cols))
    first = lax.broadcasted_iota(jnp.int32, (8, cols), 0) == 0
    control = control_ref[...]
    cost_ref[...] = folded(control * control) + jnp.where(first, line, 0.0)


def expand(small, rows, cols):
    left = lax.broadcasted_iota(jnp.int32, (rows * SUB, rows), 0) // SUB
    left = (left == lax.broadcasted_iota(jnp.int32, (rows * SUB, rows), 1)).astype(F32).astype(BF16)
    right = lax.broadcasted_iota(jnp.int32, (cols, cols * SUB), 1) // SUB
    right = (right == lax.broadcasted_iota(jnp.int32, (cols, cols * SUB), 0)).astype(F32).astype(BF16)
    wide = jnp.dot(small, right, preferred_element_type=F32).astype(BF16)
    full = jnp.dot(left, wide, preferred_element_type=F32)
    row = lax.broadcasted_iota(jnp.int32, full.shape, 0) % SUB
    col = lax.broadcasted_iota(jnp.int32, full.shape, 1) % SUB
    return jnp.where(row == col, full, 0.0).astype(BF16)


def pair_of(ref, y):
    members, _, cols = ref.shape
    blocks = [ref[:, y + k * SUB : y + (k + 1) * SUB, :].reshape(members * SUB, cols) for k in (0, 1)]
    return jnp.concatenate(blocks, axis=1)


def add_share(beta, perturbations_ref, share_ref, y):
    members = perturbations_ref.shape[0]
    cols = perturbations_ref.shape[3]
    for k in (0, 1):
        part = beta[:, k * cols : (k + 1) * cols].reshape(members, SUB, cols)
        rows = slice(y + k * SUB, y + (k + 1) * SUB)
        for c in range(3):
            term = part[0] * perturbations_ref[0, c, rows, :].astype(F32)
            for i in range(1, members):
                term = term + part[i] * perturbations_ref[i, c, rows, :].astype(F32)
            share_ref[c, rows, :] += term


def own_kernel(groups, to_beta_ref, to_grad_ref, alpha_ref, perturbations_ref, kron_beta_ref, kron_grad_ref, share_ref, square_ref):
    members, rows, cols = alpha_ref.shape
    for g in range(groups):
        kron_beta_ref[g] = expand(to_beta_ref[g], members, members)
        kron_grad_ref[g] = expand(to_grad_ref[g], members, members)
    share_ref[...] = jnp.zeros_like(share_ref)
    matrix = kron_beta_ref[0]
    square = jnp.zeros((8, cols), F32)
    for y in range(0, rows, 2 * SUB):
        alpha = pair_of(alpha_ref, y)
        square = square + folded(alpha[:, :cols] * alpha[:, :cols]) + folded(alpha[:, cols:] * alpha[:, cols:])
        hi, lo = split(alpha)
        beta = jnp.dot(matrix, hi, preferred_element_type=F32) + jnp.dot(matrix, lo, preferred_element_type=F32)
        add_share(beta, perturbations_ref, share_ref, y)
    square_ref[...] = square


def share_kernel(groups, *refs):
    others = refs[: groups - 1]
    kron_ref, perturbations_ref, own_ref, square_ref, out_ref = refs[groups - 1 :]
    _, rows, cols = own_ref.shape
    share_ref = out_ref
    for c in range(3):
        share_ref[c, :, :] = own_ref[c]
    for y in range(0, rows, 2 * SUB):
        beta = None
        for g, other in enumerate(others):
            term = jnp.dot(kron_ref[g + 1], pair_of(other, y), preferred_element_type=F32)
            beta = term if beta is None else beta + term
        add_share(beta, perturbations_ref, share_ref, y)
    out_ref[3, :8, :] = square_ref[...]


def increment_kernel(scale, halo, own_ref, other_ref, std_ref, control_ref, early_ref, inc_ref, top_ref, bottom_ref, cost_ref):
    rows = inc_ref.shape[1]
    inc = std_ref[...] * control_ref[...] + scale * (own_ref[:3] + other_ref[:3])
    inc_ref[...] = inc
    top_ref[...] = inc[:, :halo]
    bottom_ref[...] = inc[:, rows - halo :]
    cost_ref[...] = early_ref[...] + own_ref[3, :8, :] + other_ref[3, :8, :]


def lane_pack(fields, widths):
    cols = fields[0].shape[1]
    lane = lax.broadcasted_iota(jnp.int32, fields[0].shape, 1)
    left = right = None
    at = 0
    for field, width in zip(fields, widths):
        to_left = field if at == 0 else pltpu.roll(field, at, 1)
        to_right = field if at == 0 else pltpu.roll(field, cols - at, 1)
        left = to_left if left is None else jnp.where(lane >= at, to_left, left)
        right = to_right if right is None else jnp.where(lane < cols - at, to_right, right)
        at += width
    return left, right


def lane_unpack(from_right, from_left, at, width):
    cols = from_right.shape[1]
    lane = lax.broadcasted_iota(jnp.int32, from_right.shape, 1)
    if at:
        from_right = pltpu.roll(from_right, cols - at, 1)
        from_left = pltpu.roll(from_left, at, 1)
    return jnp.where(lane < width, from_right, jnp.where(lane >= cols - width, from_left, 0.0))


def tall(tile, below, above, gap):
    parts = [tile, below]
    if gap:
        parts.append(jnp.zeros((gap, tile.shape[1]), F32))
    parts.append(above)
    return jnp.concatenate(parts, axis=0)


def pack_kernel(halo, inc_ref, below_ref, above_ref, left_ref, right_ref):
    fields = [tall(inc_ref[c], below_ref[c], above_ref[c], 0) for c in range(3)]
    left_ref[...], right_ref[...] = lane_pack(fields, [halo] * 3)


def edges_kernel(steps, halo, reach, maps_ref, courant_ref, mask_ref, top_ref, bottom_ref):
    rows = courant_ref.shape[0]
    for k in range(2 * steps):
        top_ref[k * reach : (k + 1) * reach, :] = maps_ref[k, :reach, :]
        bottom_ref[k * reach : (k + 1) * reach, :] = maps_ref[k, rows - reach :, :]
    at = 2 * steps * reach
    for field in (courant_ref[...], mask_ref[...].astype(F32)):
        top_ref[at : at + halo, :] = field[:halo]
        bottom_ref[at : at + halo, :] = field[rows - halo :]
        at += halo


def static_rows(steps, halo, reach, maps_ref, courant_ref, mask_ref, below_ref, above_ref):
    def one(tile, at, size):
        return tall(tile, below_ref[at : at + size, :], above_ref[at : at + size, :], 2 * (halo - size))

    maps = [one(maps_ref[k], k * reach, reach) for k in range(2 * steps)]
    at = 2 * steps * reach
    courant = one(courant_ref[...], at, halo)
    wet = one(mask_ref[...].astype(F32), at + halo, halo)
    return maps, courant, wet


def static_pack_kernel(steps, halo, reach, maps_ref, courant_ref, mask_ref, below_ref, above_ref, left_ref, right_ref):
    maps, courant, wet = static_rows(steps, halo, reach, maps_ref, courant_ref, mask_ref, below_ref, above_ref)
    width = 2 * steps
    widths = [width] * steps + [halo]
    left_ref[0], right_ref[0] = lane_pack(maps[:steps] + [courant], widths)
    left_ref[1], right_ref[1] = lane_pack(maps[steps:] + [wet], widths)


def model_kernel(
    steps,
    halo,
    reach,
    side_ref,
    inc_ref,
    below_ref,
    above_ref,
    from_right_ref,
    from_left_ref,
    maps_ref,
    courant_ref,
    mask_ref,
    s_below_ref,
    s_above_ref,
    s_right_ref,
    s_left_ref,
    early_ref,
    std_ref,
    control_ref,
    perturbations_ref,
    lam_ref,
    control_new_ref,
    cost_ref,
    product_ref,
    source_ref,
):
    _, rows, cols = inc_ref.shape
    members = perturbations_ref.shape[0]
    height_ext = rows + 2 * halo
    width_ext = 2 * cols

    def east(x):
        return pltpu.roll(x, width_ext - 1, 1) - pltpu.roll(x, 1, 1)

    def north(x):
        return pltpu.roll(x, height_ext - 1, 0) - pltpu.roll(x, 1, 0)

    maps, courant, wet = static_rows(steps, halo, reach, maps_ref, courant_ref, mask_ref, s_below_ref, s_above_ref)
    width = 2 * steps

    def with_sides(field, right, left, at, size):
        return jnp.concatenate([field, lane_unpack(right, left, at, size)], axis=1)

    full_maps = []
    for part in (0, 1):
        for t in range(steps):
            full_maps.append(
                with_sides(maps[part * steps + t], s_right_ref[part], s_left_ref[part], t * width, width)
            )
    courant = with_sides(courant, s_right_ref[0], s_left_ref[0], steps * width, halo)
    wet = with_sides(wet, s_right_ref[1], s_left_ref[1], steps * width, halo)
    state = [
        with_sides(
            tall(inc_ref[c], below_ref[c], above_ref[c], 0), from_right_ref[...], from_left_ref[...], c * halo, halo
        )
        for c in range(3)
    ]
    row = lax.broadcasted_iota(jnp.int32, (height_ext, width_ext), 0)
    below_outside = side_ref[1] == 1
    above_outside = side_ref[0] == 1
    outside = ((row >= rows) & (row < rows + halo) & below_outside) | ((row >= rows + halo) & above_outside)
    half_inside = jnp.where(outside, 0.0, 0.5)
    half_wet = 0.5 * wet
    half_both = half_wet * courant
    height, u, v = state[0], wet * state[1], wet * state[2]
    total = early_ref[...]
    for t in range(steps):
        u = u - half_wet * east(height)
        v = v - half_wet * north(height)
        height = height - half_inside * (east(courant * u) + north(courant * v))
        source = full_maps[t] * height - full_maps[steps + t]
        source_ref[t] = source
        total = total + folded(height[:rows, :cols] * (source[:rows, :cols] - full_maps[steps + t][:rows, :cols]))
    cost_ref[...] = jnp.broadcast_to(total[None], (cost_ref.shape[0] // 8, 8, cols)).reshape(cost_ref.shape)
    adj = source_ref[steps - 1]
    adj_u = adj_v = None
    for t in range(steps - 1, -1, -1):
        if t < steps - 1:
            adj = adj + source_ref[t]
        du = half_both * east(adj)
        dv = half_both * north(adj)
        adj_u = du if adj_u is None else adj_u + du
        adj_v = dv if adj_v is None else adj_v + dv
        adj = adj + half_inside * (east(adj_u) + north(adj_v))
    lam = [x[:rows, :cols] for x in (adj, adj_u, adj_v)]
    for c in range(3):
        lam_ref[c] = lam[c]
        old = control_ref[c]
        control_new_ref[c] = old - step_length * (old + std_ref[c] * lam[c])
    for i in range(members):
        product_ref[i] = products(perturbations_ref, lam_ref, i, slice(0, rows)).astype(BF16)


def products(perturbations_ref, lam_ref, i, rows):
    total = perturbations_ref[i, 0, rows, :].astype(F32) * lam_ref[0, rows, :]
    for c in (1, 2):
        total = total + perturbations_ref[i, c, rows, :].astype(F32) * lam_ref[c, rows, :]
    return total


def base_kernel(scale, kron_ref, alpha_ref, perturbations_ref, lam_ref, out_ref, product_ref):
    members, rows, cols = alpha_ref.shape
    for i in range(members):
        product_ref[i] = products(perturbations_ref, lam_ref, i, slice(0, rows))
    matrix = kron_ref[0]
    for y in range(0, rows, 2 * SUB):
        hi, lo = split(pair_of(product_ref, y))
        grad = jnp.dot(matrix, hi, preferred_element_type=F32) + jnp.dot(matrix, lo, preferred_element_type=F32)
        for k in (0, 1):
            at = slice(y + k * SUB, y + (k + 1) * SUB)
            part = grad[:, k * cols : (k + 1) * cols].reshape(members, SUB, cols)
            old = alpha_ref[:, at, :]
            out_ref[:, at, :] = old - step_length * (old + scale * part)


def final_kernel(groups, scale, *refs):
    others = refs[: groups - 1]
    kron_ref, base_ref, out_ref = refs[groups - 1 :]
    members, rows, cols = base_ref.shape
    for y in range(0, rows, 2 * SUB):
        grad = None
        for g, other in enumerate(others):
            term = jnp.dot(kron_ref[g + 1], pair_of(other, y), preferred_element_type=F32)
            grad = term if grad is None else grad + term
        for k in (0, 1):
            at = slice(y + k * SUB, y + (k + 1) * SUB)
            part = grad[:, k * cols : (k + 1) * cols].reshape(members, SUB, cols)
            out_ref[:, at, :] = base_ref[:, at, :] - (step_length * scale) * part


def to_others(x, groups):
    return [lax.ppermute(x, "ens", [(i, (i - k) % groups) for i in range(groups)]) for k in range(1, groups)]


def body(
    perturbations,
    ens_weights,
    control,
    static_std,
    courant,
    land_mask,
    band_offsets,
    band_weights,
    obs_cells,
    obs_values,
    obs_weights,
):
    own, _, rows, cols = perturbations.shape
    groups = lax.axis_size("ens")
    n_ty, n_tx = lax.axis_size("ty"), lax.axis_size("tx")
    members = own * groups
    steps = obs_cells.shape[2]
    halo = 4 * steps
    reach = -(-2 * steps // 8) * 8
    scale = 1.0 / math.sqrt(members)
    ens_index = lax.axis_index("ens")
    down = [(i, i + 1) for i in range(n_ty - 1)]
    up = [(i + 1, i) for i in range(n_ty - 1)]
    right = [(i, (i + 1) % n_tx) for i in range(n_tx)]
    left = [(j, i) for i, j in right]

    alpha_others = to_others(ens_weights.astype(BF16), groups)

    cells, values, weights = (x.reshape(steps, x.shape[-1]) for x in (obs_cells, obs_values, obs_weights))
    maps, early = call(
        functools.partial(maps_kernel, steps),
        [((2 * steps, rows, cols), F32), ((8, cols), F32)],
        [cells, values, weights, control],
        flops=2 * steps * 4 * rows * cols * cells.shape[1],
        name="maps",
    )
    edge_rows = 2 * steps * reach + 2 * halo
    s_top, s_bottom = call(
        functools.partial(edges_kernel, steps, halo, reach),
        [((edge_rows, cols), F32)] * 2,
        [maps, courant, land_mask],
        name="edges",
    )
    s_above = lax.ppermute(s_bottom, "ty", down)
    s_below = lax.ppermute(s_top, "ty", up)
    s_to_left, s_to_right = call(
        functools.partial(static_pack_kernel, steps, halo, reach),
        [((2, rows + 2 * halo, cols), F32)] * 2,
        [maps, courant, land_mask, s_below, s_above],
        name="static_pack",
    )
    s_from_left = lax.ppermute(s_to_right, "tx", right)
    s_from_right = lax.ppermute(s_to_left, "tx", left)

    offsets = lax.dynamic_slice_in_dim(jnp.concatenate([band_offsets, band_offsets]), ens_index * own, members)
    first = ens_index * own
    index = jnp.arange(members, dtype=jnp.int32)

    def coefficients(shift):
        place = jnp.mod(shift, members)
        return jnp.sum(jnp.where(place[..., None] == index, band_weights, 0.0), axis=-1).astype(BF16)

    to_beta = coefficients(
        first + index[:own][None, :, None] - offsets.reshape(groups, own)[:, None, :]
    )
    to_grad = coefficients(
        first + index.reshape(groups, own)[:, None, :] - offsets[:own][None, :, None]
    )
    wide = own * SUB
    kron_beta, kron_grad, own_share, square = call(
        functools.partial(own_kernel, groups),
        [((groups, wide, wide), BF16)] * 2 + [((3, rows, cols), F32), ((8, cols), F32)],
        [to_beta, to_grad, ens_weights, perturbations],
        name="own",
    )
    (share,) = call(
        functools.partial(share_kernel, groups),
        [((4, rows, cols), F32)],
        [*alpha_others, kron_beta, perturbations, own_share, square],
        name="share",
    )
    if groups == 2:
        (share_other,) = to_others(share, groups)
    else:
        share = lax.psum(share, "ens")
        share_other = jnp.zeros_like(share)
    inc, top, bottom, early = call(
        functools.partial(increment_kernel, scale, halo),
        [((3, rows, cols), F32), ((3, halo, cols), F32), ((3, halo, cols), F32), ((8, cols), F32)],
        [share, share_other, static_std, control, early],
        name="increment",
    )
    above = lax.ppermute(bottom, "ty", down)
    below = lax.ppermute(top, "ty", up)
    to_left, to_right = call(
        functools.partial(pack_kernel, halo),
        [((rows + 2 * halo, cols), F32)] * 2,
        [inc, below, above],
        name="pack",
    )
    from_left = lax.ppermute(to_right, "tx", right)
    from_right = lax.ppermute(to_left, "tx", left)

    ty_index = lax.axis_index("ty")
    side = jnp.stack([ty_index == 0, ty_index == n_ty - 1]).astype(jnp.int32)
    lam, control_new, cost_terms, product = call(
        functools.partial(model_kernel, steps, halo, reach),
        [
            ((3, rows, cols), F32),
            ((3, rows, cols), F32),
            ((n_ty * n_tx * 8, cols), F32),
            ((own, rows, cols), BF16),
        ],
        [
            side,
            inc,
            below,
            above,
            from_right,
            from_left,
            maps,
            courant,
            land_mask,
            s_below,
            s_above,
            s_from_right,
            s_from_left,
            early,
            static_std,
            control,
            perturbations,
        ],
        scratch=[pltpu.VMEM((steps, rows + 2 * halo, 2 * cols), F32)],
        smem=1,
        name="model",
    )
    product_others = to_others(product, groups)
    terms = lax.all_to_all(cost_terms, ("ty", "tx"), 0, 0, tiled=True)
    cost_value = jnp.sum(terms) * (0.5 / ((3 + members) * rows * cols * n_ty * n_tx))
    (base,) = call(
        functools.partial(base_kernel, scale),
        [((own, rows, cols), F32)],
        [kron_grad, ens_weights, perturbations, lam],
        scratch=[pltpu.VMEM((own, rows, cols), F32)],
        name="base",
    )
    (weights_new,) = call(
        functools.partial(final_kernel, groups, scale),
        [((own, rows, cols), F32)],
        [*product_others, kron_grad, base],
        name="final",
    )
    return (control_new, weights_new, cost_value)


def solution(mesh):
    return jax.shard_map(
        body,
        mesh=mesh,
        in_specs=(
            P("ens", None, "ty", "tx"),
            P("ens", "ty", "tx"),
            P(None, "ty", "tx"),
            P(None, "ty", "tx"),
            P("ty", "tx"),
            P("ty", "tx"),
            P(),
            P(),
            P("ty", "tx", None, None),
            P("ty", "tx", None, None),
            P("ty", "tx", None, None),
        ),
        out_specs=(P(None, "ty", "tx"), P("ens", "ty", "tx"), P()),
        check_vma=False,
    )
```

```python
import functools
import math

import jax
import jax.numpy as jnp
from jax import lax
from jax.experimental import pallas as pl
from jax.experimental.pallas import tpu as pltpu
from jax.sharding import PartitionSpec as P

step_length = 0.25
SUB = 16
UNIT = 2 * SUB
PIECES = 3
F32 = jnp.float32
BF16 = jnp.bfloat16
VMEM = pl.BlockSpec(memory_space=pltpu.VMEM)
SMEM = pl.BlockSpec(memory_space=pltpu.SMEM)
HBM = pl.BlockSpec(memory_space=pltpu.HBM)


def call(kernel, outs, ins, scratch=(), smem=0, flops=0, name=None, mib=4, out_specs=None, in_specs=None, grid=()):
    out_shape = [jax.ShapeDtypeStruct(s, d) for s, d in outs]
    moved = sum(math.prod(s) * jnp.dtype(d).itemsize for s, d in outs)
    moved += sum(x.size * x.dtype.itemsize for x in ins)
    return pl.pallas_call(
        kernel,
        out_shape=out_shape,
        grid=grid,
        in_specs=in_specs or [SMEM] * smem + [VMEM] * (len(ins) - smem),
        out_specs=out_specs or [VMEM] * len(outs),
        scratch_shapes=list(scratch),
        compiler_params=pltpu.CompilerParams(vmem_limit_bytes=mib * 1024 * 1024),
        cost_estimate=pl.CostEstimate(flops=flops, bytes_accessed=moved, transcendentals=0),
        name=name,
    )(*ins)


def split(x):
    hi = x.astype(BF16)
    return hi, (x - hi.astype(F32)).astype(BF16)


def folded(x):
    cols = x.shape[-1]
    return jnp.sum(x.reshape(-1, 8, cols), axis=0)


def maps_kernel(steps, cells_ref, values_ref, weights_ref, control_ref, maps_ref, cost_ref):
    rows, cols = maps_ref.shape[1:]
    count = cells_ref.shape[1]
    shift = cols.bit_length() - 1
    row_iota = lax.broadcasted_iota(jnp.int32, (rows, count), 0)
    col_iota = lax.broadcasted_iota(jnp.int32, (cols, count), 0)
    for t in range(steps):
        cells = cells_ref[t : t + 1, :]
        weight = weights_ref[t : t + 1, :]
        product = weight * values_ref[t : t + 1, :]
        at_row = jnp.where(row_iota == (cells >> shift), 1.0, 0.0).astype(BF16)
        hit = col_iota == (cells & (cols - 1))
        parts = []
        for value in (weight, product):
            for piece in split(value):
                parts.append(jnp.where(hit, piece.astype(F32), 0.0).astype(BF16))
        sums = lax.dot_general(
            at_row,
            jnp.concatenate(parts, axis=0),
            (((1,), (1,)), ((), ())),
            preferred_element_type=F32,
        )
        maps_ref[t] = sums[:, :cols] + sums[:, cols : 2 * cols]
        maps_ref[steps + t] = sums[:, 2 * cols : 3 * cols] + sums[:, 3 * cols :]
    value = values_ref[...]
    fixed = jnp.sum(weights_ref[...] * value * value, axis=0, keepdims=True)
    line = sum(fixed[:, k : k + cols] for k in range(0, count, cols))
    first = lax.broadcasted_iota(jnp.int32, (8, cols), 0) == 0
    control = control_ref[...]
    cost_ref[...] = folded(control * control) + jnp.where(first, line, 0.0)


def send_kernel(chunk, alpha_ref, *refs):
    out_ref, rows_ref, sems = refs[-3:]
    copies = []
    for n, y in enumerate(chunk):
        at = slice(n * UNIT, (n + 1) * UNIT)
        copies.append(pltpu.make_async_copy(alpha_ref.at[:, y : y + UNIT, :], rows_ref.at[:, at, :], sems.at[n]))
        copies[-1].start()
    for n, copy in enumerate(copies):
        at = slice(n * UNIT, (n + 1) * UNIT)
        copy.wait()
        out_ref[:, at, :] = rows_ref[:, at, :].astype(BF16)


def expand(small):
    rows, cols = small.shape
    left = lax.broadcasted_iota(jnp.int32, (rows * SUB, rows), 0) // SUB
    left = (left == lax.broadcasted_iota(jnp.int32, (rows * SUB, rows), 1)).astype(F32).astype(BF16)
    right = lax.broadcasted_iota(jnp.int32, (cols, cols * SUB), 1) // SUB
    right = (right == lax.broadcasted_iota(jnp.int32, (cols, cols * SUB), 0)).astype(F32).astype(BF16)
    wide = jnp.dot(small, right, preferred_element_type=F32).astype(BF16)
    full = jnp.dot(left, wide, preferred_element_type=F32)
    row = lax.broadcasted_iota(jnp.int32, full.shape, 0) % SUB
    col = lax.broadcasted_iota(jnp.int32, full.shape, 1) % SUB
    return jnp.where(row == col, full, 0.0).astype(BF16)


def coefficients(own, members, axis, first_row, first_col, offsets_ref, weights_ref):
    shape = (own, own)
    row_place = lax.broadcasted_iota(jnp.int32, shape, axis)
    column = first_col + lax.broadcasted_iota(jnp.int32, shape, 1 - axis)
    shift = jnp.zeros(shape, jnp.int32)
    for j in range(own):
        shift = jnp.where(row_place == j, offsets_ref[first_row + j], shift)
    place = column - shift
    place = jnp.where(place < 0, place + members, place)
    value = jnp.zeros(shape, F32)
    for k in range(members):
        value = jnp.where(place == k, weights_ref[k], value)
    return value.astype(BF16)


def pair_of(ref, y):
    members, _, cols = ref.shape
    blocks = [ref[:, y + k * SUB : y + (k + 1) * SUB, :].reshape(members * SUB, cols) for k in (0, 1)]
    return jnp.concatenate(blocks, axis=1)


def shares(beta, perturbations_ref, y):
    members = perturbations_ref.shape[0]
    cols = perturbations_ref.shape[3]
    for k in (0, 1):
        part = beta[:, k * cols : (k + 1) * cols].reshape(members, SUB, cols)
        at = y + k * SUB
        for c in range(3):
            total = part[0] * perturbations_ref[0, c, at : at + SUB, :].astype(F32)
            for i in range(1, members):
                total = total + part[i] * perturbations_ref[i, c, at : at + SUB, :].astype(F32)
            yield k * SUB, c, total


def own_kernel(
    groups,
    place_ref,
    offsets_ref,
    weights_ref,
    alpha_hbm_ref,
    perturbations_ref,
    kron_beta_ref,
    kron_grad_ref,
    share_ref,
    square_ref,
    alpha_ref,
    sem,
):
    own, rows, cols = alpha_ref.shape
    load = pltpu.make_async_copy(alpha_hbm_ref, alpha_ref, sem)
    load.start()
    members = own * groups
    first = place_ref[2] * own
    for g in range(groups):
        other = lax.rem(place_ref[2] + g, groups) * own
        kron_beta_ref[g] = expand(coefficients(own, members, 1, other, first, offsets_ref, weights_ref))
        kron_grad_ref[g] = expand(coefficients(own, members, 0, first, other, offsets_ref, weights_ref))
    load.wait()
    matrix = kron_beta_ref[0]
    square = jnp.zeros((8, cols), F32)
    for y in range(0, rows, UNIT):
        alpha = pair_of(alpha_ref, y)
        square = square + folded(alpha[:, :cols] * alpha[:, :cols]) + folded(alpha[:, cols:] * alpha[:, cols:])
        hi, lo = split(alpha)
        beta = jnp.dot(matrix, hi, preferred_element_type=F32) + jnp.dot(matrix, lo, preferred_element_type=F32)
        for at, c, total in shares(beta, perturbations_ref, y):
            share_ref[c, y + at : y + at + SUB, :] = total
    for k in range(PIECES):
        piece = square.astype(BF16).astype(F32)
        square = square - piece
        square_ref[k * SUB : (k + 1) * SUB, :] = jnp.concatenate([piece, jnp.zeros_like(square)], axis=0).astype(BF16)


def share_kernel(groups, units, *refs):
    others = refs[: groups - 1]
    kron_ref, perturbations_ref, own_ref, out_ref = refs[groups - 1 :]
    height = len(units) * UNIT
    for n, y in enumerate(units):
        beta = None
        for g, other in enumerate(others):
            term = jnp.dot(kron_ref[g + 1], pair_of(other, n * UNIT), preferred_element_type=F32)
            beta = term if beta is None else beta + term
        for at, c, total in shares(beta, perturbations_ref, y):
            total = total + own_ref[c, y + at : y + at + SUB, :]
            to = c * height + n * UNIT + at
            out_ref[to : to + SUB, :] = total.astype(BF16)


def row_sizes(steps, halo):
    reach = [-(-2 * (t + 1) // 8) * 8 for t in range(steps)]
    return reach * 2 + [halo] * 8


def whole(rows):
    return -(-rows // SUB) * SUB


def strips_kernel(steps, halo, units, share_ref, std_ref, control_ref, maps_ref, courant_ref, mask_ref, top_ref, bottom_ref):
    rows, cols = courant_ref.shape
    height = len(units) * UNIT
    share = share_ref[...].astype(F32)
    sizes = row_sizes(steps, halo)
    for ref, low, share_low in ((top_ref, True, 0), (bottom_ref, False, height - halo)):

        def pick(size):
            return slice(0, size) if low else slice(rows - size, rows)

        fields = [maps_ref[k, pick(sizes[k]), :] for k in range(2 * steps)]
        fields += [courant_ref[pick(halo), :], mask_ref[pick(halo), :].astype(F32)]
        fields += [std_ref[c, pick(halo), :] * control_ref[c, pick(halo), :] for c in range(3)]
        fields += [share[c * height + share_low : c * height + share_low + halo] for c in range(3)]
        fill = ref.shape[0] - sum(sizes)
        if fill:
            fields.append(jnp.zeros((fill, cols), F32))
        ref[...] = jnp.concatenate(fields, axis=0).astype(BF16)


def merge_kernel(steps, halo, outer, inner, outer_ref, inner_ref, below_ref, above_ref, square_ref, out_ref):
    for units, ref in ((outer, outer_ref), (inner, inner_ref)):
        height = len(units) * UNIT
        rows = (len(outer) + len(inner)) * UNIT
        for c in range(3):
            for n, y in enumerate(units):
                at = c * height + n * UNIT
                out_ref[c * rows + y : c * rows + y + UNIT, :] = ref[at : at + UNIT, :]
    at = sum(row_sizes(steps, halo)) - 3 * halo
    beside = [ref[...].astype(F32)[at : at + 3 * halo] for ref in (below_ref, above_ref)]
    out_ref[3 * rows : 3 * rows + 6 * halo, :] = jnp.concatenate(beside, axis=0).astype(BF16)
    out_ref[3 * rows + 6 * halo :, :] = square_ref[...]


def lane_pack(fields, widths):
    cols = fields[0].shape[1]
    lane = lax.broadcasted_iota(jnp.int32, fields[0].shape, 1)
    left = right = None
    at = 0
    for field, width in zip(fields, widths):
        to_left = field if at == 0 else pltpu.roll(field, at, 1)
        to_right = field if at == 0 else pltpu.roll(field, cols - at, 1)
        left = to_left if left is None else jnp.where(lane >= at, to_left, left)
        right = to_right if right is None else jnp.where(lane < cols - at, to_right, right)
        at += width
    return left, right


def lane_unpack(from_right, from_left, at, width):
    cols = from_right.shape[1]
    lane = lax.broadcasted_iota(jnp.int32, from_right.shape, 1)
    if at:
        from_right = pltpu.roll(from_right, cols - at, 1)
        from_left = pltpu.roll(from_left, at, 1)
    return jnp.where(lane < width, from_right, jnp.where(lane >= cols - width, from_left, 0.0))


def lane_blocks(steps, halo):
    maps = [[(part * steps + t, 2 * (t + 1)) for t in range(steps)] for part in (0, 1)]
    at = 2 * steps
    return [maps[0] + [(at + 2 + c, halo) for c in range(3)], maps[1] + [(at, halo), (at + 1, halo)]]


def pack_kernel(
    steps,
    halo,
    scale,
    place_ref,
    own_ref,
    other_ref,
    std_ref,
    control_ref,
    early_ref,
    maps_ref,
    courant_ref,
    mask_ref,
    below_ref,
    above_ref,
    tall_ref,
    left_ref,
    right_ref,
    cost_ref,
):
    rows, cols = courant_ref.shape
    fields = 2 * steps + 2
    for k in range(2 * steps):
        tall_ref[k, :rows, :] = maps_ref[k]
    tall_ref[2 * steps, :rows, :] = courant_ref[...]
    tall_ref[2 * steps + 1, :rows, :] = mask_ref[...].astype(F32)
    for c in range(3):
        at = slice(c * rows, (c + 1) * rows)
        total = own_ref[at, :].astype(F32) + other_ref[at, :].astype(F32)
        tall_ref[fields + c, :rows, :] = std_ref[c] * control_ref[c] + scale * total
    at = slice(3 * rows, 3 * rows + 6 * halo)
    beside = scale * (own_ref[at, :].astype(F32) + other_ref[at, :].astype(F32))
    at = 3 * rows + 6 * halo
    squares = [
        sum(ref[at + k * SUB : at + (k + 1) * SUB, :].astype(F32) for k in range(PIECES)) for ref in (own_ref, other_ref)
    ]
    cost_ref[...] = early_ref[...] + (squares[0] + squares[1])[:8]
    sizes = row_sizes(steps, halo)
    below_outside, above_outside = place_ref[1] == 1, place_ref[0] == 1
    below, above = below_ref[...].astype(F32), above_ref[...].astype(F32)
    at = 0
    for k in range(fields + 3):
        size = sizes[k]
        lower, upper = below[at : at + size], above[at : at + size]
        if k >= fields:
            c = k - fields
            lower = lower + beside[c * halo : (c + 1) * halo]
            upper = upper + beside[(3 + c) * halo : (4 + c) * halo]
        at += size
        parts = [jnp.where(below_outside, 0.0, lower), jnp.where(above_outside, 0.0, upper)]
        if size < halo:
            parts.insert(1, jnp.zeros((2 * (halo - size), cols), F32))
        tall_ref[k, rows:, :] = jnp.concatenate(parts, axis=0)
    height = rows + 2 * halo
    for n, block in enumerate(lane_blocks(steps, halo)):
        values = [tall_ref[k] for k, _ in block]
        left, right = lane_pack(values, [w for _, w in block])
        left_ref[n * height : (n + 1) * height, :] = left.astype(BF16)
        right_ref[n * height : (n + 1) * height, :] = right.astype(BF16)


def model_kernel(
    steps,
    halo,
    place_ref,
    tall_ref,
    from_right_ref,
    from_left_ref,
    early_ref,
    std_ref,
    control_ref,
    perturbations_ref,
    control_new_ref,
    cost_out_ref,
    product_ref,
    source_ref,
    lam_ref,
    cost_ref,
    cost_sem,
):
    _, rows, cols = control_ref.shape
    members = perturbations_ref.shape[0]
    height_ext = rows + 2 * halo
    width_ext = 2 * cols

    def east(x):
        return pltpu.roll(x, width_ext - 1, 1) - pltpu.roll(x, 1, 1)

    def north(x):
        return pltpu.roll(x, height_ext - 1, 0) - pltpu.roll(x, 1, 0)

    fields = 2 * steps + 2
    sides = {}
    for n, block in enumerate(lane_blocks(steps, halo)):
        at = 0
        from_right = from_right_ref[n * height_ext : (n + 1) * height_ext, :].astype(F32)
        from_left = from_left_ref[n * height_ext : (n + 1) * height_ext, :].astype(F32)
        for k, size in block:
            sides[k] = lane_unpack(from_right, from_left, at, size)
            at += size
    full = [jnp.concatenate([tall_ref[k], sides[k]], axis=1) for k in range(fields + 3)]
    courant, wet = full[2 * steps : fields]
    row = lax.broadcasted_iota(jnp.int32, (height_ext, width_ext), 0)
    outside = ((row >= rows) & (row < rows + halo) & (place_ref[1] == 1)) | ((row >= rows + halo) & (place_ref[0] == 1))
    half_inside = jnp.where(outside, 0.0, 0.5)
    half_wet = 0.5 * wet
    half_both = half_wet * courant
    height, u, v = full[fields], wet * full[fields + 1], wet * full[fields + 2]
    total = early_ref[...]
    for t in range(steps):
        u = u - half_wet * east(height)
        v = v - half_wet * north(height)
        height = height - half_inside * (east(courant * u) + north(courant * v))
        offset = full[steps + t]
        source = full[t] * height - offset
        source_ref[t] = source
        total = total + folded(height[:rows, :cols] * (source[:rows, :cols] - offset[:rows, :cols]))
    cost_ref[...] = jnp.broadcast_to(total[None], (cost_ref.shape[0] // 8, 8, cols)).reshape(cost_ref.shape)
    cost_copy = pltpu.make_async_copy(cost_ref, cost_out_ref, cost_sem)
    cost_copy.start()
    adj = source_ref[steps - 1]
    adj_u = adj_v = None
    for t in range(steps - 1, -1, -1):
        if t < steps - 1:
            adj = adj + source_ref[t]
        du = half_both * east(adj)
        dv = half_both * north(adj)
        adj_u = du if adj_u is None else adj_u + du
        adj_v = dv if adj_v is None else adj_v + dv
        adj = adj + half_inside * (east(adj_u) + north(adj_v))
    lam = [x[:rows, :cols] for x in (adj, adj_u, adj_v)]
    for c in range(3):
        lam_ref[c] = lam[c]
        old = control_ref[c]
        control_new_ref[c] = old - step_length * (old + std_ref[c] * lam[c])
    for i in range(members):
        product_ref[i] = products(perturbations_ref, lam_ref, i).astype(BF16)
    cost_copy.wait()


def products(perturbations_ref, lam_ref, i):
    total = perturbations_ref[i, 0].astype(F32) * lam_ref[0]
    for c in (1, 2):
        total = total + perturbations_ref[i, c].astype(F32) * lam_ref[c]
    return total


def final_kernel(groups, scale, cost_scale, *refs):
    parts = refs[:groups]
    kron_ref, alpha_ref, terms_ref, out_ref, cost_ref = refs[groups:]
    members, rows, cols = alpha_ref.shape
    cost_ref[0, 0] = jnp.sum(terms_ref[...]) * cost_scale
    for y in range(0, rows, UNIT):
        grad = None
        for g, part in enumerate(parts):
            term = jnp.dot(kron_ref[g], pair_of(part, y), preferred_element_type=F32)
            grad = term if grad is None else grad + term
        for k in (0, 1):
            at = slice(y + k * SUB, y + (k + 1) * SUB)
            part = grad[:, k * cols : (k + 1) * cols].reshape(members, SUB, cols)
            old = alpha_ref[:, at, :]
            out_ref[:, at, :] = old - step_length * (old + scale * part)


def to_others(x, groups):
    return [lax.ppermute(x, "ens", [(i, (i - k) % groups) for i in range(groups)]) for k in range(1, groups)]


def sum_parts(share, groups):
    if groups == 2:
        return share, to_others(share, groups)[0]
    share = lax.psum(share.astype(F32), "ens")
    return share, jnp.zeros_like(share)


def body(
    perturbations,
    ens_weights,
    control,
    static_std,
    courant,
    land_mask,
    band_offsets,
    band_weights,
    obs_cells,
    obs_values,
    obs_weights,
):
    own, _, rows, cols = perturbations.shape
    groups = lax.axis_size("ens")
    n_ty, n_tx = lax.axis_size("ty"), lax.axis_size("tx")
    members = own * groups
    steps = obs_cells.shape[2]
    halo = 4 * steps
    scale = 1.0 / math.sqrt(members)
    down = [(i, (i + 1) % n_ty) for i in range(n_ty)]
    up = [(j, i) for i, j in down]
    right = [(i, (i + 1) % n_tx) for i in range(n_tx)]
    left = [(j, i) for i, j in right]
    ty_index = lax.axis_index("ty")
    place = jnp.stack(
        [
            (ty_index == 0).astype(jnp.int32),
            (ty_index == n_ty - 1).astype(jnp.int32),
            lax.axis_index("ens").astype(jnp.int32),
        ]
    )
    units = list(range(0, rows, UNIT))
    at_edge = -(-halo // UNIT)
    outer = units[:at_edge] + units[len(units) - at_edge :]
    inner = units[at_edge : len(units) - at_edge]

    def rows_of(chunk, mib, *before):
        shape = (own, len(chunk) * UNIT, cols)
        (sent,) = call(
            functools.partial(send_kernel, chunk),
            [(shape, BF16)],
            [ens_weights, *before],
            in_specs=[HBM] * (1 + len(before)),
            scratch=[pltpu.VMEM(shape, F32), pltpu.SemaphoreType.DMA((len(chunk),))],
            name="send",
            mib=mib,
        )
        return sent

    outer_sent = rows_of(outer, 56)
    outer_others = to_others(outer_sent, groups)
    inner_others = to_others(rows_of(inner, 4, outer_sent), groups)

    cells, values, weights = (x.reshape(steps, x.shape[-1]) for x in (obs_cells, obs_values, obs_weights))
    maps, early = call(
        functools.partial(maps_kernel, steps),
        [((2 * steps, rows, cols), F32), ((8, cols), F32)],
        [cells, values, weights, control],
        flops=2 * steps * 4 * rows * cols * cells.shape[1],
        name="maps",
    )
    wide = own * SUB
    kron_beta, kron_grad, own_share, square = call(
        functools.partial(own_kernel, groups),
        [((groups, wide, wide), BF16)] * 2 + [((3, rows, cols), F32), ((PIECES * SUB, cols), BF16)],
        [place, band_offsets, band_weights, ens_weights, perturbations],
        in_specs=[SMEM, SMEM, SMEM, HBM, VMEM],
        scratch=[pltpu.VMEM((own, rows, cols), F32), pltpu.SemaphoreType.DMA],
        name="own",
    )

    def share_of(units, others, name):
        (share,) = call(
            functools.partial(share_kernel, groups, units),
            [((3 * len(units) * UNIT, cols), BF16)],
            [*others, kron_beta, perturbations, own_share],
            name=name,
        )
        return share

    outer_share = share_of(outer, outer_others, "outer_share")
    edge_rows = whole(sum(row_sizes(steps, halo)))
    top, bottom = call(
        functools.partial(strips_kernel, steps, halo, outer),
        [((edge_rows, cols), BF16)] * 2,
        [outer_share, static_std, control, maps, courant, land_mask],
        name="strips",
    )
    above = lax.ppermute(bottom, "ty", down)
    below = lax.ppermute(top, "ty", up)

    inner_share = share_of(inner, inner_others, "inner_share")
    (share,) = call(
        functools.partial(merge_kernel, steps, halo, outer, inner),
        [((3 * rows + 6 * halo + PIECES * SUB, cols), BF16)],
        [outer_share, inner_share, below, above, square],
        name="merge",
    )
    share, share_other = sum_parts(share, groups)
    high = rows + 2 * halo
    tall, to_left, to_right, early = call(
        functools.partial(pack_kernel, steps, halo, scale),
        [((2 * steps + 5, high, cols), F32), ((2 * high, cols), BF16), ((2 * high, cols), BF16), ((8, cols), F32)],
        [place, share, share_other, static_std, control, early, maps, courant, land_mask, below, above],
        smem=1,
        name="pack",
    )
    from_left = lax.ppermute(to_right, "tx", right)
    from_right = lax.ppermute(to_left, "tx", left)

    control_new, cost_terms, product = call(
        functools.partial(model_kernel, steps, halo),
        [
            ((3, rows, cols), F32),
            ((n_ty * n_tx * 8, cols), F32),
            ((own, rows, cols), BF16),
        ],
        [place, tall, from_right, from_left, early, static_std, control, perturbations],
        scratch=[
            pltpu.VMEM((steps, high, 2 * cols), F32),
            pltpu.VMEM((3, rows, cols), F32),
            pltpu.VMEM((n_ty * n_tx * 8, cols), F32),
            pltpu.SemaphoreType.DMA,
        ],
        out_specs=[VMEM, HBM, VMEM],
        smem=1,
        mib=16,
        name="model",
    )
    product_others = to_others(product, groups)
    terms = lax.all_to_all(cost_terms, ("ty", "tx"), 0, 0, tiled=True)
    cost_scale = 0.5 / ((3 + members) * rows * cols * n_ty * n_tx)

    weights_new, cost = call(
        functools.partial(final_kernel, groups, scale, cost_scale),
        [((own, rows, cols), F32), ((1, 1), F32)],
        [product, *product_others, kron_grad, ens_weights, terms],
        out_specs=[VMEM, SMEM],
        name="final",
    )
    return (control_new, weights_new, cost.reshape(()))


def solution(mesh):
    return jax.shard_map(
        body,
        mesh=mesh,
        in_specs=(
            P("ens", None, "ty", "tx"),
            P("ens", "ty", "tx"),
            P(None, "ty", "tx"),
            P(None, "ty", "tx"),
            P("ty", "tx"),
            P("ty", "tx"),
            P(),
            P(),
            P("ty", "tx", None, None),
            P("ty", "tx", None, None),
            P("ty", "tx", None, None),
        ),
        out_specs=(P(None, "ty", "tx"), P("ens", "ty", "tx"), P()),
        check_vma=False,
    )
```

```python
import functools
import math

import jax
import jax.numpy as jnp
from jax import lax
from jax.experimental import pallas as pl
from jax.experimental.pallas import tpu as pltpu
from jax.sharding import PartitionSpec as P

step_length = 0.25
SUB = 16
UNIT = 2 * SUB
PIECES = 3
ROW = 8
GROUP = 24
F32 = jnp.float32
BF16 = jnp.bfloat16
VMEM = pl.BlockSpec(memory_space=pltpu.VMEM)
SMEM = pl.BlockSpec(memory_space=pltpu.SMEM)
HBM = pl.BlockSpec(memory_space=pltpu.HBM)


def call(kernel, outs, ins, scratch=(), smem=0, flops=0, name=None, mib=4, out_specs=None, in_specs=None, grid=()):
    out_shape = [jax.ShapeDtypeStruct(s, d) for s, d in outs]
    moved = sum(math.prod(s) * jnp.dtype(d).itemsize for s, d in outs)
    moved += sum(x.size * x.dtype.itemsize for x in ins)
    return pl.pallas_call(
        kernel,
        out_shape=out_shape,
        grid=grid,
        in_specs=in_specs or [SMEM] * smem + [VMEM] * (len(ins) - smem),
        out_specs=out_specs or [VMEM] * len(outs),
        scratch_shapes=list(scratch),
        compiler_params=pltpu.CompilerParams(vmem_limit_bytes=mib * 1024 * 1024),
        cost_estimate=pl.CostEstimate(flops=flops, bytes_accessed=moved, transcendentals=0),
        name=name,
    )(*ins)


def split(x):
    hi = x.astype(BF16)
    return hi, (x - hi.astype(F32)).astype(BF16)


def folded(x):
    cols = x.shape[-1]
    return jnp.sum(x.reshape(-1, 8, cols), axis=0)


def maps_kernel(steps, cells_ref, values_ref, weights_ref, control_ref, maps_ref, cost_ref):
    rows, cols = maps_ref.shape[1:]
    count = cells_ref.shape[1]
    shift = cols.bit_length() - 1
    row_iota = lax.broadcasted_iota(jnp.int32, (rows, count), 0)
    col_iota = lax.broadcasted_iota(jnp.int32, (cols, count), 0)
    for t in range(steps):
        cells = cells_ref[t : t + 1, :]
        weight = weights_ref[t : t + 1, :]
        product = weight * values_ref[t : t + 1, :]
        at_row = jnp.where(row_iota == (cells >> shift), 1.0, 0.0).astype(BF16)
        hit = col_iota == (cells & (cols - 1))
        parts = []
        for value in (weight, product):
            for piece in split(value):
                parts.append(jnp.where(hit, piece.astype(F32), 0.0).astype(BF16))
        sums = lax.dot_general(
            at_row,
            jnp.concatenate(parts, axis=0),
            (((1,), (1,)), ((), ())),
            preferred_element_type=F32,
        )
        maps_ref[t] = sums[:, :cols] + sums[:, cols : 2 * cols]
        maps_ref[steps + t] = sums[:, 2 * cols : 3 * cols] + sums[:, 3 * cols :]
    value = values_ref[...]
    fixed = jnp.sum(weights_ref[...] * value * value, axis=0, keepdims=True)
    line = sum(fixed[:, k : k + cols] for k in range(0, count, cols))
    first = lax.broadcasted_iota(jnp.int32, (8, cols), 0) == 0
    control = control_ref[...]
    cost_ref[...] = folded(control * control) + jnp.where(first, line, 0.0)


def send_kernel(chunk, alpha_ref, *refs):
    out_ref, rows_ref, sems = refs[-3:]
    copies = []
    for n, y in enumerate(chunk):
        at = slice(n * UNIT, (n + 1) * UNIT)
        copies.append(pltpu.make_async_copy(alpha_ref.at[:, y : y + UNIT, :], rows_ref.at[:, at, :], sems.at[n]))
        copies[-1].start()
    for n, copy in enumerate(copies):
        at = slice(n * UNIT, (n + 1) * UNIT)
        copy.wait()
        out_ref[:, at, :] = rows_ref[:, at, :].astype(BF16)


def expand(small):
    rows, cols = small.shape
    left = lax.broadcasted_iota(jnp.int32, (rows * SUB, rows), 0) // SUB
    left = (left == lax.broadcasted_iota(jnp.int32, (rows * SUB, rows), 1)).astype(F32).astype(BF16)
    right = lax.broadcasted_iota(jnp.int32, (cols, cols * SUB), 1) // SUB
    right = (right == lax.broadcasted_iota(jnp.int32, (cols, cols * SUB), 0)).astype(F32).astype(BF16)
    wide = jnp.dot(small, right, preferred_element_type=F32).astype(BF16)
    full = jnp.dot(left, wide, preferred_element_type=F32)
    row = lax.broadcasted_iota(jnp.int32, full.shape, 0) % SUB
    col = lax.broadcasted_iota(jnp.int32, full.shape, 1) % SUB
    return jnp.where(row == col, full, 0.0).astype(BF16)


def coefficients(own, members, axis, first_row, first_col, offsets_ref, weights_ref):
    shape = (own, own)
    row_place = lax.broadcasted_iota(jnp.int32, shape, axis)
    column = first_col + lax.broadcasted_iota(jnp.int32, shape, 1 - axis)
    shift = jnp.zeros(shape, jnp.int32)
    for j in range(own):
        shift = jnp.where(row_place == j, offsets_ref[first_row + j], shift)
    place = column - shift
    place = jnp.where(place < 0, place + members, place)
    value = jnp.zeros(shape, F32)
    for k in range(members):
        value = jnp.where(place == k, weights_ref[k], value)
    return value.astype(BF16)


def pair_of(ref, y):
    members, _, cols = ref.shape
    blocks = [ref[:, y + k * SUB : y + (k + 1) * SUB, :].reshape(members * SUB, cols) for k in (0, 1)]
    return jnp.concatenate(blocks, axis=1)


def shares(beta, perturbations_ref, y):
    members = perturbations_ref.shape[0]
    cols = perturbations_ref.shape[3]
    for k in (0, 1):
        part = beta[:, k * cols : (k + 1) * cols].reshape(members, SUB, cols)
        at = y + k * SUB
        for c in range(3):
            total = part[0] * perturbations_ref[0, c, at : at + SUB, :].astype(F32)
            for i in range(1, members):
                total = total + part[i] * perturbations_ref[i, c, at : at + SUB, :].astype(F32)
            yield k * SUB, c, total


def own_kernel(
    groups,
    place_ref,
    offsets_ref,
    weights_ref,
    alpha_hbm_ref,
    perturbations_ref,
    kron_beta_ref,
    kron_grad_ref,
    share_ref,
    square_ref,
    alpha_ref,
    sem,
):
    own, rows, cols = alpha_ref.shape
    load = pltpu.make_async_copy(alpha_hbm_ref, alpha_ref, sem)
    load.start()
    members = own * groups
    first = place_ref[2] * own
    for g in range(groups):
        other = lax.rem(place_ref[2] + g, groups) * own
        kron_beta_ref[g] = expand(coefficients(own, members, 1, other, first, offsets_ref, weights_ref))
        kron_grad_ref[g] = expand(coefficients(own, members, 0, first, other, offsets_ref, weights_ref))
    load.wait()
    matrix = kron_beta_ref[0]
    square = jnp.zeros((8, cols), F32)
    for y in range(0, rows, UNIT):
        alpha = pair_of(alpha_ref, y)
        square = square + folded(alpha[:, :cols] * alpha[:, :cols]) + folded(alpha[:, cols:] * alpha[:, cols:])
        hi, lo = split(alpha)
        beta = jnp.dot(matrix, hi, preferred_element_type=F32) + jnp.dot(matrix, lo, preferred_element_type=F32)
        for at, c, total in shares(beta, perturbations_ref, y):
            share_ref[c, y + at : y + at + SUB, :] = total
    for k in range(PIECES):
        piece = square.astype(BF16).astype(F32)
        square = square - piece
        square_ref[k * SUB : (k + 1) * SUB, :] = jnp.concatenate([piece, jnp.zeros_like(square)], axis=0).astype(BF16)


def share_kernel(groups, units, *refs):
    others = refs[: groups - 1]
    kron_ref, perturbations_ref, own_ref, out_ref = refs[groups - 1 :]
    height = len(units) * UNIT
    for n, y in enumerate(units):
        beta = None
        for g, other in enumerate(others):
            term = jnp.dot(kron_ref[g + 1], pair_of(other, n * UNIT), preferred_element_type=F32)
            beta = term if beta is None else beta + term
        for at, c, total in shares(beta, perturbations_ref, y):
            total = total + own_ref[c, y + at : y + at + SUB, :]
            to = c * height + n * UNIT + at
            out_ref[to : to + SUB, :] = total.astype(BF16)


def row_sizes(steps, halo):
    reach = [-(-2 * (t + 1) // 8) * 8 for t in range(steps)]
    return reach * 2 + [halo] * 8


def whole(rows):
    return -(-rows // SUB) * SUB


def strips_kernel(steps, halo, units, share_ref, std_ref, control_ref, maps_ref, courant_ref, mask_ref, top_ref, bottom_ref):
    rows, cols = courant_ref.shape
    height = len(units) * UNIT
    share = share_ref[...].astype(F32)
    sizes = row_sizes(steps, halo)
    for ref, low, share_low in ((top_ref, True, 0), (bottom_ref, False, height - halo)):

        def pick(size):
            return slice(0, size) if low else slice(rows - size, rows)

        fields = [maps_ref[k, pick(sizes[k]), :] for k in range(2 * steps)]
        fields += [courant_ref[pick(halo), :], mask_ref[pick(halo), :].astype(F32)]
        fields += [std_ref[c, pick(halo), :] * control_ref[c, pick(halo), :] for c in range(3)]
        fields += [share[c * height + share_low : c * height + share_low + halo] for c in range(3)]
        fill = ref.shape[0] - sum(sizes)
        if fill:
            fields.append(jnp.zeros((fill, cols), F32))
        ref[...] = jnp.concatenate(fields, axis=0).astype(BF16)


def merge_kernel(steps, halo, outer, inner, outer_ref, inner_ref, below_ref, above_ref, square_ref, out_ref):
    for units, ref in ((outer, outer_ref), (inner, inner_ref)):
        height = len(units) * UNIT
        rows = (len(outer) + len(inner)) * UNIT
        for c in range(3):
            for n, y in enumerate(units):
                at = c * height + n * UNIT
                out_ref[c * rows + y : c * rows + y + UNIT, :] = ref[at : at + UNIT, :]
    at = sum(row_sizes(steps, halo)) - 3 * halo
    beside = [ref[...].astype(F32)[at : at + 3 * halo] for ref in (below_ref, above_ref)]
    out_ref[3 * rows : 3 * rows + 6 * halo, :] = jnp.concatenate(beside, axis=0).astype(BF16)
    out_ref[3 * rows + 6 * halo :, :] = square_ref[...]


def lane_pack(fields, widths):
    cols = fields[0].shape[1]
    lane = lax.broadcasted_iota(jnp.int32, fields[0].shape, 1)
    left = right = None
    at = 0
    for field, width in zip(fields, widths):
        to_left = field if at == 0 else pltpu.roll(field, at, 1)
        to_right = field if at == 0 else pltpu.roll(field, cols - at, 1)
        left = to_left if left is None else jnp.where(lane >= at, to_left, left)
        right = to_right if right is None else jnp.where(lane < cols - at, to_right, right)
        at += width
    return left, right


def lane_unpack(from_right, from_left, at, width):
    cols = from_right.shape[1]
    lane = lax.broadcasted_iota(jnp.int32, from_right.shape, 1)
    if at:
        from_right = pltpu.roll(from_right, cols - at, 1)
        from_left = pltpu.roll(from_left, at, 1)
    return jnp.where(lane < width, from_right, jnp.where(lane >= cols - width, from_left, 0.0))


def lane_blocks(steps, halo):
    maps = [[(part * steps + t, 2 * (t + 1)) for t in range(steps)] for part in (0, 1)]
    at = 2 * steps
    return [maps[0] + [(at + 2 + c, halo) for c in range(3)], maps[1] + [(at, halo), (at + 1, halo)]]


def pack_kernel(
    steps,
    halo,
    scale,
    place_ref,
    own_ref,
    other_ref,
    std_ref,
    control_ref,
    early_ref,
    maps_ref,
    courant_ref,
    mask_ref,
    below_ref,
    above_ref,
    tall_ref,
    left_ref,
    right_ref,
    cost_ref,
):
    rows, cols = courant_ref.shape
    fields = 2 * steps + 2
    for k in range(2 * steps):
        tall_ref[k, :rows, :] = maps_ref[k]
    tall_ref[2 * steps, :rows, :] = courant_ref[...]
    tall_ref[2 * steps + 1, :rows, :] = mask_ref[...].astype(F32)
    for c in range(3):
        at = slice(c * rows, (c + 1) * rows)
        total = own_ref[at, :].astype(F32) + other_ref[at, :].astype(F32)
        tall_ref[fields + c, :rows, :] = std_ref[c] * control_ref[c] + scale * total
    at = slice(3 * rows, 3 * rows + 6 * halo)
    beside = scale * (own_ref[at, :].astype(F32) + other_ref[at, :].astype(F32))
    at = 3 * rows + 6 * halo
    squares = [
        sum(ref[at + k * SUB : at + (k + 1) * SUB, :].astype(F32) for k in range(PIECES)) for ref in (own_ref, other_ref)
    ]
    cost_ref[...] = early_ref[...] + (squares[0] + squares[1])[:8]
    sizes = row_sizes(steps, halo)
    below_outside, above_outside = place_ref[1] == 1, place_ref[0] == 1
    below, above = below_ref[...].astype(F32), above_ref[...].astype(F32)
    at = 0
    for k in range(fields + 3):
        size = sizes[k]
        lower, upper = below[at : at + size], above[at : at + size]
        if k >= fields:
            c = k - fields
            lower = lower + beside[c * halo : (c + 1) * halo]
            upper = upper + beside[(3 + c) * halo : (4 + c) * halo]
        at += size
        parts = [jnp.where(below_outside, 0.0, lower), jnp.where(above_outside, 0.0, upper)]
        if size < halo:
            parts.insert(1, jnp.zeros((2 * (halo - size), cols), F32))
        tall_ref[k, rows:, :] = jnp.concatenate(parts, axis=0)
    height = rows + 2 * halo
    for n, block in enumerate(lane_blocks(steps, halo)):
        values = [tall_ref[k] for k, _ in block]
        left, right = lane_pack(values, [w for _, w in block])
        left_ref[n * height : (n + 1) * height, :] = left.astype(BF16)
        right_ref[n * height : (n + 1) * height, :] = right.astype(BF16)


def model_kernel(
    steps,
    halo,
    place_ref,
    tall_ref,
    from_right_ref,
    from_left_ref,
    early_ref,
    std_ref,
    control_ref,
    control_new_ref,
    cost_out_ref,
    lam_ref,
    source_ref,
    cost_ref,
    cost_sem,
    sides_ref,
    courant_ref,
    half_wet_ref,
    half_both_ref,
    *state_refs,
):
    _, rows, cols = control_ref.shape
    height_ext = rows + 2 * halo
    fields = 2 * steps + 2
    tile, extra, total_blocks = rows // ROW, halo // ROW, height_ext // ROW
    states = state_refs[:3], state_refs[3:]
    left, right = slice(0, cols), slice(cols, 2 * cols)
    row = lax.broadcasted_iota(jnp.int32, (ROW, 2 * cols), 0)
    top, last = row == 0, row == ROW - 1
    half = [jnp.where(place_ref[k] == 1, 0.0, 0.5) for k in (0, 1)]

    def at(k):
        k = k % total_blocks
        return slice(k * ROW, (k + 1) * ROW)

    def half_inside(k):
        return half[0] if k < 0 else half[1] if k >= tile else 0.5

    def around(reach):
        n = min(extra, -(-reach // ROW))
        return range(-n, tile + n)

    def east(x):
        return pltpu.roll(x, 2 * cols - 1, 1) - pltpu.roll(x, 1, 1)

    class Column:
        def __init__(self):
            self.value, self.up, self.down = {}, {}, {}

        def put(self, k, x):
            self.value[k], self.up[k], self.down[k] = x, pltpu.roll(x, ROW - 1, 0), pltpu.roll(x, 1, 0)

        def north(self, k):
            up = jnp.where(last, self.up.get(k + 1, self.up[k]), self.up[k])
            return up - jnp.where(top, self.down.get(k - 1, self.down[k]), self.down[k])

    for n, block in enumerate(lane_blocks(steps, halo)):
        place = 0
        from_right = from_right_ref[n * height_ext : (n + 1) * height_ext, :].astype(F32)
        from_left = from_left_ref[n * height_ext : (n + 1) * height_ext, :].astype(F32)
        for k, size in block:
            sides_ref[k] = lane_unpack(from_right, from_left, place, size)
            place += size

    def joined(k, rows_at):
        return jnp.concatenate([tall_ref[k, rows_at, :], sides_ref[k, rows_at, :]], axis=1)

    for k in around(halo):
        wet, courant = joined(2 * steps + 1, at(k)), joined(2 * steps, at(k))
        half_wet_ref[at(k), :] = 0.5 * wet
        courant_ref[at(k), :] = courant
        half_both_ref[at(k), :] = 0.5 * wet * courant
        states[0][0][at(k), :] = joined(fields, at(k))
        states[0][1][at(k), :] = wet * joined(fields + 1, at(k))
        states[0][2][at(k), :] = wet * joined(fields + 2, at(k))

    total = early_ref[...]
    for t in range(steps):
        out = halo - 2 * (t + 1)
        src, dst = states[t % 2], states[1 - t % 2]
        flow, result, seen = around(out + 1), around(out), around(2 * (t + 1))
        height, flux, spread = Column(), Column(), {}
        for k in (flow[0] - 1, flow[0]):
            if k >= -extra:
                height.put(k, src[0][at(k), :])
        for first in range(flow[0], flow[-1] + 2, GROUP):
            group = [k for k in range(first, first + GROUP) if k in flow]
            for k in group:
                if k + 1 < tile + extra:
                    height.put(k + 1, src[0][at(k + 1), :])
            slopes = [(east(height.value[k]), height.north(k)) for k in group]
            moved = []
            for k, (x, y) in zip(group, slopes):
                half_wet = half_wet_ref[at(k), :]
                moved.append((src[1][at(k), :] - half_wet * x, src[2][at(k), :] - half_wet * y))
            for k, (u, v) in zip(group, moved):
                dst[1][at(k), :] = u
                dst[2][at(k), :] = v
            flows = []
            for k, (u, v) in zip(group, moved):
                courant = courant_ref[at(k), :]
                flows.append((courant * u, courant * v))
            for k, (u, v) in zip(group, flows):
                spread[k] = east(u)
                flux.put(k, v)
            ready = [k for k in range(first - 1, first + GROUP - 1) if k in result]
            new = [height.value[k] - half_inside(k) * (spread[k] + flux.north(k)) for k in ready]
            for k, x in zip(ready, new):
                dst[0][at(k), :] = x
            for k, x in zip(ready, new):
                if k in seen:
                    offset = joined(steps + t, at(k))
                    source = joined(t, at(k)) * x - offset
                    source_ref[t, at(k), :] = source
                    if 0 <= k < tile:
                        total = total + x[:, left] * (source[:, left] - offset[:, left])
    cost_ref[...] = jnp.broadcast_to(total[None], (cost_ref.shape[0] // 8, 8, cols)).reshape(cost_ref.shape)
    cost_copy = pltpu.make_async_copy(cost_ref, cost_out_ref, cost_sem)
    cost_copy.start()

    for t in range(steps - 1, -1, -1):
        given, flow, result = around(2 * (t + 1)), around(2 * t + 1), around(2 * t)
        src, dst = states[t % 2], states[1 - t % 2]
        adj, flux, spread, east_flow = Column(), Column(), {}, {}

        def load(k):
            x = source_ref[t, at(k), :]
            adj.put(k, x if t == steps - 1 else x + src[0][at(k), :])

        for k in (flow[0] - 1, flow[0]):
            if k in given:
                load(k)
        for first in range(flow[0], flow[-1] + 2, GROUP):
            group = [k for k in range(first, first + GROUP) if k in flow]
            for k in group:
                if k + 1 in given:
                    load(k + 1)
            slopes = [(east(adj.value[k]), adj.north(k)) for k in group]
            moved = []
            for k, (x, y) in zip(group, slopes):
                half_both = half_both_ref[at(k), :]
                u, v = half_both * x, half_both * y
                if t < steps - 1:
                    u = u + src[1][at(k), :]
                    v = v + src[2][at(k), :]
                moved.append((u, v))
            for k, (u, v) in zip(group, moved):
                spread[k] = east(u)
                flux.put(k, v)
            for k, (u, v) in zip(group, moved):
                if t:
                    dst[1][at(k), :] = u
                    dst[2][at(k), :] = v
                elif 0 <= k < tile:
                    lam_ref[1, at(k), :] = u[:, left]
                    lam_ref[2, at(k), :] = v[:, left]
            ready = [k for k in range(first - 1, first + GROUP - 1) if k in result]
            new = [adj.value[k] + half_inside(k) * (spread[k] + flux.north(k)) for k in ready]
            for k, x in zip(ready, new):
                if t:
                    dst[0][at(k), :] = x
                else:
                    lam_ref[0, at(k), :] = x[:, left]
    for c in range(3):
        old = control_ref[c]
        control_new_ref[c] = old - step_length * (old + std_ref[c] * lam_ref[c])
    cost_copy.wait()


def model_scratch(steps, halo, rows, cols, terms):
    high = rows + 2 * halo
    return [
        pltpu.VMEM((steps, high, 2 * cols), F32),
        pltpu.VMEM((terms, cols), F32),
        pltpu.SemaphoreType.DMA,
        pltpu.VMEM((2 * steps + 5, high, cols), F32),
    ] + [pltpu.VMEM((high, 2 * cols), F32)] * 9


def products_kernel(units, ahead, lam_ref, perturbations_ref, *refs):
    count = (len(refs) - 2) // 2
    others, sent_ref, ahead_refs = refs[:count], refs[count], refs[count + 1 :]

    def products(ref, i, at, rows):
        total = ref[i, 0, at, :].astype(F32) * lam_ref[0, rows, :]
        for c in (1, 2):
            total = total + ref[i, c, at, :].astype(F32) * lam_ref[c, rows, :]
        return total.astype(BF16)

    for i in range(perturbations_ref.shape[0]):
        for n, y in enumerate(units):
            rows = slice(y, y + UNIT)
            sent_ref[i, n * UNIT : (n + 1) * UNIT, :] = products(perturbations_ref, i, rows, rows)
        for n, y in enumerate(ahead):
            rows, at = slice(y, y + UNIT), slice(n * UNIT, (n + 1) * UNIT)
            ahead_refs[0][i, at, :] = products(perturbations_ref, i, rows, rows)
            for ref, out_ref in zip(others, ahead_refs[1:]):
                out_ref[i, at, :] = products(ref, i, at, rows)


def final_kernel(groups, scale, cost_scale, units, ahead, *refs):
    late, early = refs[:groups], refs[groups : 2 * groups]
    kron_ref, alpha_ref, terms_ref, out_ref, cost_ref = refs[2 * groups :]
    members, rows, cols = alpha_ref.shape
    cost_ref[0, 0] = jnp.sum(terms_ref[...]) * cost_scale
    for parts, chunk in ((early, ahead), (late, units)):
        for n, y in enumerate(chunk):
            grad = None
            for g, part in enumerate(parts):
                term = jnp.dot(kron_ref[g], pair_of(part, n * UNIT), preferred_element_type=F32)
                grad = term if grad is None else grad + term
            for k in (0, 1):
                at = slice(y + k * SUB, y + (k + 1) * SUB)
                part = grad[:, k * cols : (k + 1) * cols].reshape(members, SUB, cols)
                old = alpha_ref[:, at, :]
                out_ref[:, at, :] = old - step_length * (old + scale * part)


def to_others(x, groups):
    return [lax.ppermute(x, "ens", [(i, (i - k) % groups) for i in range(groups)]) for k in range(1, groups)]


def sum_parts(share, groups):
    if groups == 2:
        return share, to_others(share, groups)[0]
    share = lax.psum(share.astype(F32), "ens")
    return share, jnp.zeros_like(share)


def body(
    perturbations,
    ens_weights,
    control,
    static_std,
    courant,
    land_mask,
    band_offsets,
    band_weights,
    obs_cells,
    obs_values,
    obs_weights,
):
    own, _, rows, cols = perturbations.shape
    groups = lax.axis_size("ens")
    n_ty, n_tx = lax.axis_size("ty"), lax.axis_size("tx")
    members = own * groups
    steps = obs_cells.shape[2]
    halo = 4 * steps
    scale = 1.0 / math.sqrt(members)
    down = [(i, (i + 1) % n_ty) for i in range(n_ty)]
    up = [(j, i) for i, j in down]
    right = [(i, (i + 1) % n_tx) for i in range(n_tx)]
    left = [(j, i) for i, j in right]
    ty_index = lax.axis_index("ty")
    place = jnp.stack(
        [
            (ty_index == 0).astype(jnp.int32),
            (ty_index == n_ty - 1).astype(jnp.int32),
            lax.axis_index("ens").astype(jnp.int32),
        ]
    )
    units = list(range(0, rows, UNIT))
    at_edge = -(-halo // UNIT)
    outer = units[:at_edge] + units[len(units) - at_edge :]
    inner = units[at_edge : len(units) - at_edge]
    ahead = inner[: len(units) // 4]
    behind = [y for y in units if y not in ahead]

    def rows_of(chunk, mib, *before):
        shape = (own, len(chunk) * UNIT, cols)
        (sent,) = call(
            functools.partial(send_kernel, chunk),
            [(shape, BF16)],
            [ens_weights, *before],
            in_specs=[HBM] * (1 + len(before)),
            scratch=[pltpu.VMEM(shape, F32), pltpu.SemaphoreType.DMA((len(chunk),))],
            name="send",
            mib=mib,
        )
        return sent

    outer_sent = rows_of(outer, 56)
    outer_others = to_others(outer_sent, groups)
    inner_others = to_others(rows_of(inner, 4, outer_sent), groups)

    cells, values, weights = (x.reshape(steps, x.shape[-1]) for x in (obs_cells, obs_values, obs_weights))
    maps, early = call(
        functools.partial(maps_kernel, steps),
        [((2 * steps, rows, cols), F32), ((8, cols), F32)],
        [cells, values, weights, control],
        flops=2 * steps * 4 * rows * cols * cells.shape[1],
        name="maps",
    )
    wide = own * SUB
    kron_beta, kron_grad, own_share, square = call(
        functools.partial(own_kernel, groups),
        [((groups, wide, wide), BF16)] * 2 + [((3, rows, cols), F32), ((PIECES * SUB, cols), BF16)],
        [place, band_offsets, band_weights, ens_weights, perturbations],
        in_specs=[SMEM, SMEM, SMEM, HBM, VMEM],
        scratch=[pltpu.VMEM((own, rows, cols), F32), pltpu.SemaphoreType.DMA],
        name="own",
    )

    def share_of(units, others, name):
        (share,) = call(
            functools.partial(share_kernel, groups, units),
            [((3 * len(units) * UNIT, cols), BF16)],
            [*others, kron_beta, perturbations, own_share],
            name=name,
        )
        return share

    outer_share = share_of(outer, outer_others, "outer_share")
    edge_rows = whole(sum(row_sizes(steps, halo)))
    top, bottom = call(
        functools.partial(strips_kernel, steps, halo, outer),
        [((edge_rows, cols), BF16)] * 2,
        [outer_share, static_std, control, maps, courant, land_mask],
        name="strips",
    )
    above = lax.ppermute(bottom, "ty", down)
    below = lax.ppermute(top, "ty", up)

    inner_share = share_of(inner, inner_others, "inner_share")
    (share,) = call(
        functools.partial(merge_kernel, steps, halo, outer, inner),
        [((3 * rows + 6 * halo + PIECES * SUB, cols), BF16)],
        [outer_share, inner_share, below, above, square],
        name="merge",
    )
    share, share_other = sum_parts(share, groups)
    high = rows + 2 * halo
    tall, to_left, to_right, early = call(
        functools.partial(pack_kernel, steps, halo, scale),
        [((2 * steps + 5, high, cols), F32), ((2 * high, cols), BF16), ((2 * high, cols), BF16), ((8, cols), F32)],
        [place, share, share_other, static_std, control, early, maps, courant, land_mask, below, above],
        smem=1,
        name="pack",
    )
    from_left = lax.ppermute(to_right, "tx", right)
    from_right = lax.ppermute(to_left, "tx", left)

    rows_ahead = jnp.concatenate([perturbations[:, :, y : y + UNIT] for y in ahead], axis=2)
    rows_ahead, tall = lax.optimization_barrier((rows_ahead, tall))
    ahead_others = to_others(rows_ahead, groups)

    control_new, cost_terms, lam = call(
        functools.partial(model_kernel, steps, halo),
        [((3, rows, cols), F32), ((n_ty * n_tx * 8, cols), F32), ((3, rows, cols), F32)],
        [place, tall, from_right, from_left, early, static_std, control],
        scratch=model_scratch(steps, halo, rows, cols, n_ty * n_tx * 8),
        out_specs=[VMEM, HBM, VMEM],
        smem=1,
        mib=16,
        name="model",
    )
    sent, *products_ahead = call(
        functools.partial(products_kernel, behind, ahead),
        [((own, len(behind) * UNIT, cols), BF16)] + [((own, len(ahead) * UNIT, cols), BF16)] * groups,
        [lam, perturbations, *ahead_others],
        name="products",
    )
    sent_others = to_others(sent, groups)
    terms = lax.all_to_all(cost_terms, ("ty", "tx"), 0, 0, tiled=True)
    cost_scale = 0.5 / ((3 + members) * rows * cols * n_ty * n_tx)
    weights_new, cost = call(
        functools.partial(final_kernel, groups, scale, cost_scale, behind, ahead),
        [((own, rows, cols), F32), ((1, 1), F32)],
        [sent, *sent_others, *products_ahead, kron_grad, ens_weights, terms],
        out_specs=[VMEM, SMEM],
        name="final",
    )
    return (control_new, weights_new, cost.reshape(()))


def solution(mesh):
    return jax.shard_map(
        body,
        mesh=mesh,
        in_specs=(
            P("ens", None, "ty", "tx"),
            P("ens", "ty", "tx"),
            P(None, "ty", "tx"),
            P(None, "ty", "tx"),
            P("ty", "tx"),
            P("ty", "tx"),
            P(),
            P(),
            P("ty", "tx", None, None),
            P("ty", "tx", None, None),
            P("ty", "tx", None, None),
        ),
        out_specs=(P(None, "ty", "tx"), P("ens", "ty", "tx"), P()),
        check_vma=False,
    )
```

```python
import functools
import math

import jax
import jax.numpy as jnp
from jax import lax
from jax.experimental import pallas as pl
from jax.experimental.pallas import tpu as pltpu
from jax.sharding import PartitionSpec as P

step_length = 0.25
SUB = 16
UNIT = 2 * SUB
PIECES = 3
ROW = 8
GROUP = 24
F32 = jnp.float32
BF16 = jnp.bfloat16
VMEM = pl.BlockSpec(memory_space=pltpu.VMEM)
SMEM = pl.BlockSpec(memory_space=pltpu.SMEM)
HBM = pl.BlockSpec(memory_space=pltpu.HBM)


def call(kernel, outs, ins, scratch=(), smem=0, flops=0, name=None, mib=4, out_specs=None, in_specs=None, grid=()):
    out_shape = [jax.ShapeDtypeStruct(s, d) for s, d in outs]
    moved = sum(math.prod(s) * jnp.dtype(d).itemsize for s, d in outs)
    moved += sum(x.size * x.dtype.itemsize for x in ins)
    return pl.pallas_call(
        kernel,
        out_shape=out_shape,
        grid=grid,
        in_specs=in_specs or [SMEM] * smem + [VMEM] * (len(ins) - smem),
        out_specs=out_specs or [VMEM] * len(outs),
        scratch_shapes=list(scratch),
        compiler_params=pltpu.CompilerParams(vmem_limit_bytes=mib * 1024 * 1024),
        cost_estimate=pl.CostEstimate(flops=flops, bytes_accessed=moved, transcendentals=0),
        name=name,
    )(*ins)


def split(x):
    hi = x.astype(BF16)
    return hi, (x - hi.astype(F32)).astype(BF16)


def folded(x):
    cols = x.shape[-1]
    return jnp.sum(x.reshape(-1, 8, cols), axis=0)


def maps_kernel(steps, cells_ref, values_ref, weights_ref, control_ref, maps_ref, cost_ref):
    rows, cols = maps_ref.shape[1:]
    count = cells_ref.shape[1]
    shift = cols.bit_length() - 1
    row_iota = lax.broadcasted_iota(jnp.int32, (rows, count), 0)
    col_iota = lax.broadcasted_iota(jnp.int32, (cols, count), 0)
    for t in range(steps):
        cells = cells_ref[t : t + 1, :]
        weight = weights_ref[t : t + 1, :]
        product = weight * values_ref[t : t + 1, :]
        at_row = jnp.where(row_iota == (cells >> shift), 1.0, 0.0).astype(BF16)
        hit = col_iota == (cells & (cols - 1))
        parts = []
        for value in (weight, product):
            for piece in split(value):
                parts.append(jnp.where(hit, piece.astype(F32), 0.0).astype(BF16))
        sums = lax.dot_general(
            at_row,
            jnp.concatenate(parts, axis=0),
            (((1,), (1,)), ((), ())),
            preferred_element_type=F32,
        )
        maps_ref[t] = sums[:, :cols] + sums[:, cols : 2 * cols]
        maps_ref[steps + t] = sums[:, 2 * cols : 3 * cols] + sums[:, 3 * cols :]
    value = values_ref[...]
    fixed = jnp.sum(weights_ref[...] * value * value, axis=0, keepdims=True)
    line = sum(fixed[:, k : k + cols] for k in range(0, count, cols))
    first = lax.broadcasted_iota(jnp.int32, (8, cols), 0) == 0
    control = control_ref[...]
    cost_ref[...] = folded(control * control) + jnp.where(first, line, 0.0)


def send_kernel(chunk, alpha_ref, *refs):
    out_ref, rows_ref, sems = refs[-3:]
    copies = []
    for n, y in enumerate(chunk):
        at = slice(n * UNIT, (n + 1) * UNIT)
        copies.append(pltpu.make_async_copy(alpha_ref.at[:, y : y + UNIT, :], rows_ref.at[:, at, :], sems.at[n]))
        copies[-1].start()
    for n, copy in enumerate(copies):
        at = slice(n * UNIT, (n + 1) * UNIT)
        copy.wait()
        out_ref[:, at, :] = rows_ref[:, at, :].astype(BF16)


def expand(small):
    rows, cols = small.shape
    left = lax.broadcasted_iota(jnp.int32, (rows * SUB, rows), 0) // SUB
    left = (left == lax.broadcasted_iota(jnp.int32, (rows * SUB, rows), 1)).astype(F32).astype(BF16)
    right = lax.broadcasted_iota(jnp.int32, (cols, cols * SUB), 1) // SUB
    right = (right == lax.broadcasted_iota(jnp.int32, (cols, cols * SUB), 0)).astype(F32).astype(BF16)
    wide = jnp.dot(small, right, preferred_element_type=F32).astype(BF16)
    full = jnp.dot(left, wide, preferred_element_type=F32)
    row = lax.broadcasted_iota(jnp.int32, full.shape, 0) % SUB
    col = lax.broadcasted_iota(jnp.int32, full.shape, 1) % SUB
    return jnp.where(row == col, full, 0.0).astype(BF16)


def coefficients(own, members, axis, first_row, first_col, offsets_ref, weights_ref):
    shape = (own, own)
    row_place = lax.broadcasted_iota(jnp.int32, shape, axis)
    column = first_col + lax.broadcasted_iota(jnp.int32, shape, 1 - axis)
    shift = jnp.zeros(shape, jnp.int32)
    for j in range(own):
        shift = jnp.where(row_place == j, offsets_ref[first_row + j], shift)
    place = column - shift
    place = jnp.where(place < 0, place + members, place)
    value = jnp.zeros(shape, F32)
    for k in range(members):
        value = jnp.where(place == k, weights_ref[k], value)
    return value.astype(BF16)


def pair_of(ref, y):
    members, _, cols = ref.shape
    blocks = [ref[:, y + k * SUB : y + (k + 1) * SUB, :].reshape(members * SUB, cols) for k in (0, 1)]
    return jnp.concatenate(blocks, axis=1)


def shares(beta, perturbations_ref, y):
    members = perturbations_ref.shape[0]
    cols = perturbations_ref.shape[3]
    for k in (0, 1):
        part = beta[:, k * cols : (k + 1) * cols].reshape(members, SUB, cols)
        at = y + k * SUB
        for c in range(3):
            total = part[0] * perturbations_ref[0, c, at : at + SUB, :].astype(F32)
            for i in range(1, members):
                total = total + part[i] * perturbations_ref[i, c, at : at + SUB, :].astype(F32)
            yield k * SUB, c, total


def own_kernel(
    groups,
    place_ref,
    offsets_ref,
    weights_ref,
    alpha_hbm_ref,
    perturbations_ref,
    kron_beta_ref,
    kron_grad_ref,
    share_ref,
    square_ref,
    alpha_ref,
    sem,
):
    own, rows, cols = alpha_ref.shape
    load = pltpu.make_async_copy(alpha_hbm_ref, alpha_ref, sem)
    load.start()
    members = own * groups
    first = place_ref[2] * own
    for g in range(groups):
        other = lax.rem(place_ref[2] + g, groups) * own
        kron_beta_ref[g] = expand(coefficients(own, members, 1, other, first, offsets_ref, weights_ref))
        kron_grad_ref[g] = expand(coefficients(own, members, 0, first, other, offsets_ref, weights_ref))
    load.wait()
    matrix = kron_beta_ref[0]
    square = jnp.zeros((8, cols), F32)
    for y in range(0, rows, UNIT):
        alpha = pair_of(alpha_ref, y)
        square = square + folded(alpha[:, :cols] * alpha[:, :cols]) + folded(alpha[:, cols:] * alpha[:, cols:])
        hi, lo = split(alpha)
        beta = jnp.dot(matrix, hi, preferred_element_type=F32) + jnp.dot(matrix, lo, preferred_element_type=F32)
        for at, c, total in shares(beta, perturbations_ref, y):
            share_ref[c, y + at : y + at + SUB, :] = total
    rest = jnp.sum(square, axis=0, keepdims=True)
    pieces = []
    for _ in range(PIECES):
        pieces.append(rest.astype(BF16).astype(F32))
        rest = rest - pieces[-1]
    pieces.append(jnp.zeros((SUB - PIECES, cols), F32))
    square_ref[...] = jnp.concatenate(pieces, axis=0).astype(BF16)


def share_kernel(groups, units, *refs):
    others = refs[: groups - 1]
    kron_ref, perturbations_ref, own_ref, out_ref = refs[groups - 1 :]
    height = len(units) * UNIT
    for n, y in enumerate(units):
        beta = None
        for g, other in enumerate(others):
            term = jnp.dot(kron_ref[g + 1], pair_of(other, n * UNIT), preferred_element_type=F32)
            beta = term if beta is None else beta + term
        for at, c, total in shares(beta, perturbations_ref, y):
            total = total + own_ref[c, y + at : y + at + SUB, :]
            to = c * height + n * UNIT + at
            out_ref[to : to + SUB, :] = total.astype(BF16)


def row_sizes(steps, halo):
    reach = [-(-2 * (t + 1) // 8) * 8 for t in range(steps)]
    return reach * 2 + [halo] * 8


def whole(rows):
    return -(-rows // SUB) * SUB


def strips_kernel(steps, halo, units, share_ref, std_ref, control_ref, maps_ref, courant_ref, mask_ref, top_ref, bottom_ref):
    rows, cols = courant_ref.shape
    height = len(units) * UNIT
    share = share_ref[...].astype(F32)
    sizes = row_sizes(steps, halo)
    for ref, low, share_low in ((top_ref, True, 0), (bottom_ref, False, height - halo)):

        def pick(size):
            return slice(0, size) if low else slice(rows - size, rows)

        fields = [maps_ref[k, pick(sizes[k]), :] for k in range(2 * steps)]
        fields += [courant_ref[pick(halo), :], mask_ref[pick(halo), :].astype(F32)]
        fields += [std_ref[c, pick(halo), :] * control_ref[c, pick(halo), :] for c in range(3)]
        fields += [share[c * height + share_low : c * height + share_low + halo] for c in range(3)]
        fill = ref.shape[0] - sum(sizes)
        if fill:
            fields.append(jnp.zeros((fill, cols), F32))
        ref[...] = jnp.concatenate(fields, axis=0).astype(BF16)


def merge_kernel(steps, halo, outer, inner, outer_ref, inner_ref, below_ref, above_ref, square_ref, out_ref):
    for units, ref in ((outer, outer_ref), (inner, inner_ref)):
        height = len(units) * UNIT
        rows = (len(outer) + len(inner)) * UNIT
        for c in range(3):
            for n, y in enumerate(units):
                at = c * height + n * UNIT
                out_ref[c * rows + y : c * rows + y + UNIT, :] = ref[at : at + UNIT, :]
    at = sum(row_sizes(steps, halo)) - 3 * halo
    beside = [ref[...].astype(F32)[at : at + 3 * halo] for ref in (below_ref, above_ref)]
    out_ref[3 * rows : 3 * rows + 6 * halo, :] = jnp.concatenate(beside, axis=0).astype(BF16)
    out_ref[3 * rows + 6 * halo :, :] = square_ref[...]


def lane_pack(fields, widths, at=0, left=None, right=None):
    cols = fields[0].shape[1]
    lane = lax.broadcasted_iota(jnp.int32, fields[0].shape, 1)
    for field, width in zip(fields, widths):
        to_left = field if at == 0 else pltpu.roll(field, at, 1)
        to_right = field if at == 0 else pltpu.roll(field, cols - at, 1)
        left = to_left if left is None else jnp.where(lane >= at, to_left, left)
        right = to_right if right is None else jnp.where(lane < cols - at, to_right, right)
        at += width
    return left, right


def lane_unpack(from_right, from_left, at, width):
    cols = from_right.shape[1]
    lane = lax.broadcasted_iota(jnp.int32, from_right.shape, 1)
    if at:
        from_right = pltpu.roll(from_right, cols - at, 1)
        from_left = pltpu.roll(from_left, at, 1)
    return jnp.where(lane < width, from_right, jnp.where(lane >= cols - width, from_left, 0.0))


def lane_blocks(steps, halo):
    maps = [[(part * steps + t, 2 * (t + 1)) for t in range(steps)] for part in (0, 1)]
    at = 2 * steps
    return [maps[0] + [(at + 2 + c, halo) for c in range(3)], maps[1] + [(at, halo), (at + 1, halo)]]


def tall_rows(place_ref, tile, lower, upper, halo, out_ref):
    rows, cols = tile.shape
    size = lower.shape[0]
    parts = [jnp.where(place_ref[1] == 1, 0.0, lower), jnp.where(place_ref[0] == 1, 0.0, upper)]
    if size < halo:
        parts.insert(1, jnp.zeros((2 * (halo - size), cols), F32))
    out_ref[:rows, :] = tile
    out_ref[rows:, :] = jnp.concatenate(parts, axis=0)


def static_pack_kernel(
    steps, halo, place_ref, maps_ref, courant_ref, mask_ref, below_ref, above_ref, tall_ref, left_ref, right_ref
):
    sizes = row_sizes(steps, halo)
    fields = 2 * steps + 2
    below, above = below_ref[...].astype(F32), above_ref[...].astype(F32)
    at = 0
    for k in range(fields):
        tile = maps_ref[k] if k < 2 * steps else courant_ref[...] if k == 2 * steps else mask_ref[...].astype(F32)
        end = at + sizes[k]
        tall_rows(place_ref, tile, below[at:end], above[at:end], halo, tall_ref.at[k])
        at = end
    high = tall_ref.shape[1]
    for n, block in enumerate(lane_blocks(steps, halo)):
        kept = [(k, w) for k, w in block if k < fields]
        left, right = lane_pack([tall_ref[k] for k, _ in kept], [w for _, w in kept])
        left_ref[n * high : (n + 1) * high, :] = left.astype(BF16)
        right_ref[n * high : (n + 1) * high, :] = right.astype(BF16)


def pack_kernel(
    steps,
    halo,
    scale,
    place_ref,
    own_ref,
    other_ref,
    std_ref,
    control_ref,
    early_ref,
    below_ref,
    above_ref,
    static_left_ref,
    static_right_ref,
    inc_ref,
    left_ref,
    right_ref,
    cost_ref,
):
    _, rows, cols = control_ref.shape
    at = slice(3 * rows, 3 * rows + 6 * halo)
    beside = scale * (own_ref[at, :].astype(F32) + other_ref[at, :].astype(F32))
    at = 3 * rows + 6 * halo
    squares = own_ref[at : at + SUB, :].astype(F32) + other_ref[at : at + SUB, :].astype(F32)
    cost_ref[...] = early_ref[...] + squares[:8]
    below, above = below_ref[...].astype(F32), above_ref[...].astype(F32)
    first = sum(row_sizes(steps, halo)[: 2 * steps + 2])
    for c in range(3):
        at = slice(c * rows, (c + 1) * rows)
        total = own_ref[at, :].astype(F32) + other_ref[at, :].astype(F32)
        at = slice(first + c * halo, first + (c + 1) * halo)
        lower = below[at] + beside[c * halo : (c + 1) * halo]
        upper = above[at] + beside[(3 + c) * halo : (4 + c) * halo]
        tall_rows(place_ref, std_ref[c] * control_ref[c] + scale * total, lower, upper, halo, inc_ref.at[c])
    high = rows + 2 * halo
    taken = sum(2 * (t + 1) for t in range(steps))
    left, right = lane_pack(
        [inc_ref[c] for c in range(3)],
        [halo] * 3,
        taken,
        static_left_ref[:high, :].astype(F32),
        static_right_ref[:high, :].astype(F32),
    )
    left_ref[:high, :] = left.astype(BF16)
    right_ref[:high, :] = right.astype(BF16)
    left_ref[high:, :] = static_left_ref[high:, :]
    right_ref[high:, :] = static_right_ref[high:, :]


def model_kernel(
    steps,
    halo,
    place_ref,
    tall_ref,
    inc_ref,
    from_right_ref,
    from_left_ref,
    early_ref,
    std_ref,
    control_ref,
    control_new_ref,
    cost_out_ref,
    lam_ref,
    source_ref,
    cost_ref,
    cost_sem,
    sides_ref,
    courant_ref,
    half_wet_ref,
    half_both_ref,
    *state_refs,
):
    _, rows, cols = control_ref.shape
    height_ext = rows + 2 * halo
    fields = 2 * steps + 2
    tile, extra, total_blocks = rows // ROW, halo // ROW, height_ext // ROW
    states = state_refs[:3], state_refs[3:]
    left, right = slice(0, cols), slice(cols, 2 * cols)
    row = lax.broadcasted_iota(jnp.int32, (ROW, 2 * cols), 0)
    top, last = row == 0, row == ROW - 1
    half = [jnp.where(place_ref[k] == 1, 0.0, 0.5) for k in (0, 1)]

    def at(k):
        k = k % total_blocks
        return slice(k * ROW, (k + 1) * ROW)

    def half_inside(k):
        return half[0] if k < 0 else half[1] if k >= tile else 0.5

    def around(reach):
        n = min(extra, -(-reach // ROW))
        return range(-n, tile + n)

    def east(x):
        return pltpu.roll(x, 2 * cols - 1, 1) - pltpu.roll(x, 1, 1)

    class Column:
        def __init__(self):
            self.value, self.up, self.down = {}, {}, {}

        def put(self, k, x):
            self.value[k], self.up[k], self.down[k] = x, pltpu.roll(x, ROW - 1, 0), pltpu.roll(x, 1, 0)

        def north(self, k):
            up = jnp.where(last, self.up.get(k + 1, self.up[k]), self.up[k])
            return up - jnp.where(top, self.down.get(k - 1, self.down[k]), self.down[k])

    for n, block in enumerate(lane_blocks(steps, halo)):
        place = 0
        from_right = from_right_ref[n * height_ext : (n + 1) * height_ext, :].astype(F32)
        from_left = from_left_ref[n * height_ext : (n + 1) * height_ext, :].astype(F32)
        for k, size in block:
            sides_ref[k] = lane_unpack(from_right, from_left, place, size)
            place += size

    def joined(k, rows_at):
        main = tall_ref[k, rows_at, :] if k < fields else inc_ref[k - fields, rows_at, :]
        return jnp.concatenate([main, sides_ref[k, rows_at, :]], axis=1)

    for k in around(halo):
        wet, courant = joined(2 * steps + 1, at(k)), joined(2 * steps, at(k))
        half_wet_ref[at(k), :] = 0.5 * wet
        courant_ref[at(k), :] = courant
        half_both_ref[at(k), :] = 0.5 * wet * courant
        states[0][0][at(k), :] = joined(fields, at(k))
        states[0][1][at(k), :] = wet * joined(fields + 1, at(k))
        states[0][2][at(k), :] = wet * joined(fields + 2, at(k))

    total = early_ref[...]
    for t in range(steps):
        out = halo - 2 * (t + 1)
        src, dst = states[t % 2], states[1 - t % 2]
        flow, result, seen = around(out + 1), around(out), around(2 * (t + 1))
        height, flux, spread = Column(), Column(), {}
        for k in (flow[0] - 1, flow[0]):
            if k >= -extra:
                height.put(k, src[0][at(k), :])
        for first in range(flow[0], flow[-1] + 2, GROUP):
            group = [k for k in range(first, first + GROUP) if k in flow]
            for k in group:
                if k + 1 < tile + extra:
                    height.put(k + 1, src[0][at(k + 1), :])
            slopes = [(east(height.value[k]), height.north(k)) for k in group]
            moved = []
            for k, (x, y) in zip(group, slopes):
                half_wet = half_wet_ref[at(k), :]
                moved.append((src[1][at(k), :] - half_wet * x, src[2][at(k), :] - half_wet * y))
            for k, (u, v) in zip(group, moved):
                dst[1][at(k), :] = u
                dst[2][at(k), :] = v
            flows = []
            for k, (u, v) in zip(group, moved):
                courant = courant_ref[at(k), :]
                flows.append((courant * u, courant * v))
            for k, (u, v) in zip(group, flows):
                spread[k] = east(u)
                flux.put(k, v)
            ready = [k for k in range(first - 1, first + GROUP - 1) if k in result]
            new = [height.value[k] - half_inside(k) * (spread[k] + flux.north(k)) for k in ready]
            for k, x in zip(ready, new):
                dst[0][at(k), :] = x
            for k, x in zip(ready, new):
                if k in seen:
                    offset = joined(steps + t, at(k))
                    source = joined(t, at(k)) * x - offset
                    source_ref[t, at(k), :] = source
                    if 0 <= k < tile:
                        total = total + x[:, left] * (source[:, left] - offset[:, left])
    cost_ref[...] = jnp.broadcast_to(jnp.sum(total, axis=0, keepdims=True), cost_ref.shape)
    cost_copy = pltpu.make_async_copy(cost_ref, cost_out_ref, cost_sem)
    cost_copy.start()

    for t in range(steps - 1, -1, -1):
        given, flow, result = around(2 * (t + 1)), around(2 * t + 1), around(2 * t)
        src, dst = states[t % 2], states[1 - t % 2]
        adj, flux, spread, east_flow = Column(), Column(), {}, {}

        def load(k):
            x = source_ref[t, at(k), :]
            adj.put(k, x if t == steps - 1 else x + src[0][at(k), :])

        for k in (flow[0] - 1, flow[0]):
            if k in given:
                load(k)
        for first in range(flow[0], flow[-1] + 2, GROUP):
            group = [k for k in range(first, first + GROUP) if k in flow]
            for k in group:
                if k + 1 in given:
                    load(k + 1)
            slopes = [(east(adj.value[k]), adj.north(k)) for k in group]
            moved = []
            for k, (x, y) in zip(group, slopes):
                half_both = half_both_ref[at(k), :]
                u, v = half_both * x, half_both * y
                if t < steps - 1:
                    u = u + src[1][at(k), :]
                    v = v + src[2][at(k), :]
                moved.append((u, v))
            for k, (u, v) in zip(group, moved):
                spread[k] = east(u)
                flux.put(k, v)
            for k, (u, v) in zip(group, moved):
                if t:
                    dst[1][at(k), :] = u
                    dst[2][at(k), :] = v
                elif 0 <= k < tile:
                    lam_ref[1, at(k), :] = u[:, left]
                    lam_ref[2, at(k), :] = v[:, left]
            ready = [k for k in range(first - 1, first + GROUP - 1) if k in result]
            new = [adj.value[k] + half_inside(k) * (spread[k] + flux.north(k)) for k in ready]
            for k, x in zip(ready, new):
                if t:
                    dst[0][at(k), :] = x
                else:
                    lam_ref[0, at(k), :] = x[:, left]
    for c in range(3):
        old = control_ref[c]
        control_new_ref[c] = old - step_length * (old + std_ref[c] * lam_ref[c])
    cost_copy.wait()


def model_scratch(steps, halo, rows, cols, terms):
    high = rows + 2 * halo
    return [
        pltpu.VMEM((steps, high, 2 * cols), F32),
        pltpu.VMEM((terms, cols), F32),
        pltpu.SemaphoreType.DMA,
        pltpu.VMEM((2 * steps + 5, high, cols), F32),
    ] + [pltpu.VMEM((high, 2 * cols), F32)] * 9


def ahead_kernel(ahead, perturbations_ref, early_ref, out_ref):
    for n, y in enumerate(ahead):
        out_ref[:, :, n * UNIT : (n + 1) * UNIT, :] = perturbations_ref[:, :, y : y + UNIT, :]


def products_kernel(units, ahead, lam_ref, perturbations_ref, *refs):
    count = (len(refs) - 2) // 2
    others, sent_ref, ahead_refs = refs[:count], refs[count], refs[count + 1 :]

    def products(ref, i, at, rows):
        total = ref[i, 0, at, :].astype(F32) * lam_ref[0, rows, :]
        for c in (1, 2):
            total = total + ref[i, c, at, :].astype(F32) * lam_ref[c, rows, :]
        return total.astype(BF16)

    for i in range(perturbations_ref.shape[0]):
        for n, y in enumerate(units):
            rows = slice(y, y + UNIT)
            sent_ref[i, n * UNIT : (n + 1) * UNIT, :] = products(perturbations_ref, i, rows, rows)
        for n, y in enumerate(ahead):
            rows, at = slice(y, y + UNIT), slice(n * UNIT, (n + 1) * UNIT)
            ahead_refs[0][i, at, :] = products(perturbations_ref, i, rows, rows)
            for ref, out_ref in zip(others, ahead_refs[1:]):
                out_ref[i, at, :] = products(ref, i, at, rows)


def final_kernel(groups, scale, cost_scale, units, ahead, *refs):
    late, early = refs[:groups], refs[groups : 2 * groups]
    kron_ref, alpha_ref, terms_ref, out_ref, cost_ref = refs[2 * groups :]
    members, rows, cols = alpha_ref.shape
    cost_ref[0, 0] = jnp.sum(terms_ref[...]) * cost_scale
    for parts, chunk in ((early, ahead), (late, units)):
        for n, y in enumerate(chunk):
            grad = None
            for g, part in enumerate(parts):
                term = jnp.dot(kron_ref[g], pair_of(part, n * UNIT), preferred_element_type=F32)
                grad = term if grad is None else grad + term
            for k in (0, 1):
                at = slice(y + k * SUB, y + (k + 1) * SUB)
                part = grad[:, k * cols : (k + 1) * cols].reshape(members, SUB, cols)
                old = alpha_ref[:, at, :]
                out_ref[:, at, :] = old - step_length * (old + scale * part)


def to_others(x, groups):
    return [lax.ppermute(x, "ens", [(i, (i - k) % groups) for i in range(groups)]) for k in range(1, groups)]


def sum_parts(share, groups):
    if groups == 2:
        return share, to_others(share, groups)[0]
    share = lax.psum(share.astype(F32), "ens")
    return share, jnp.zeros_like(share)


def body(
    perturbations,
    ens_weights,
    control,
    static_std,
    courant,
    land_mask,
    band_offsets,
    band_weights,
    obs_cells,
    obs_values,
    obs_weights,
):
    own, _, rows, cols = perturbations.shape
    groups = lax.axis_size("ens")
    n_ty, n_tx = lax.axis_size("ty"), lax.axis_size("tx")
    members = own * groups
    steps = obs_cells.shape[2]
    halo = 4 * steps
    scale = 1.0 / math.sqrt(members)
    down = [(i, (i + 1) % n_ty) for i in range(n_ty)]
    up = [(j, i) for i, j in down]
    right = [(i, (i + 1) % n_tx) for i in range(n_tx)]
    left = [(j, i) for i, j in right]
    ty_index = lax.axis_index("ty")
    place = jnp.stack(
        [
            (ty_index == 0).astype(jnp.int32),
            (ty_index == n_ty - 1).astype(jnp.int32),
            lax.axis_index("ens").astype(jnp.int32),
        ]
    )
    units = list(range(0, rows, UNIT))
    at_edge = -(-halo // UNIT)
    outer = units[:at_edge] + units[len(units) - at_edge :]
    inner = units[at_edge : len(units) - at_edge]
    ahead = inner[: len(units) // 4]
    behind = [y for y in units if y not in ahead]

    def rows_of(chunk, mib, *before):
        shape = (own, len(chunk) * UNIT, cols)
        (sent,) = call(
            functools.partial(send_kernel, chunk),
            [(shape, BF16)],
            [ens_weights, *before],
            in_specs=[HBM] * (1 + len(before)),
            scratch=[pltpu.VMEM(shape, F32), pltpu.SemaphoreType.DMA((len(chunk),))],
            name="send",
            mib=mib,
        )
        return sent

    outer_sent = rows_of(outer, 56)
    outer_others = to_others(outer_sent, groups)

    cells, values, weights = (x.reshape(steps, x.shape[-1]) for x in (obs_cells, obs_values, obs_weights))
    maps, early = call(
        functools.partial(maps_kernel, steps),
        [((2 * steps, rows, cols), F32), ((8, cols), F32)],
        [cells, values, weights, control],
        flops=2 * steps * 4 * rows * cols * cells.shape[1],
        name="maps",
    )
    wide = own * SUB
    kron_beta, kron_grad, own_share, square = call(
        functools.partial(own_kernel, groups),
        [((groups, wide, wide), BF16)] * 2 + [((3, rows, cols), F32), ((SUB, cols), BF16)],
        [place, band_offsets, band_weights, ens_weights, perturbations],
        in_specs=[SMEM, SMEM, SMEM, HBM, VMEM],
        scratch=[pltpu.VMEM((own, rows, cols), F32), pltpu.SemaphoreType.DMA],
        name="own",
    )

    inner_others = to_others(rows_of(inner, 4, square), groups)

    def share_of(units, others, name):
        (share,) = call(
            functools.partial(share_kernel, groups, units),
            [((3 * len(units) * UNIT, cols), BF16)],
            [*others, kron_beta, perturbations, own_share],
            name=name,
        )
        return share

    outer_share = share_of(outer, outer_others, "outer_share")
    edge_rows = whole(sum(row_sizes(steps, halo)))
    top, bottom = call(
        functools.partial(strips_kernel, steps, halo, outer),
        [((edge_rows, cols), BF16)] * 2,
        [outer_share, static_std, control, maps, courant, land_mask],
        name="strips",
    )
    above = lax.ppermute(bottom, "ty", down)
    below = lax.ppermute(top, "ty", up)

    inner_share = share_of(inner, inner_others, "inner_share")
    (share,) = call(
        functools.partial(merge_kernel, steps, halo, outer, inner),
        [((3 * rows + 6 * halo + SUB, cols), BF16)],
        [outer_share, inner_share, below, above, square],
        name="merge",
    )
    share, share_other = sum_parts(share, groups)
    high = rows + 2 * halo
    packed = [((2 * high, cols), BF16)] * 2
    tall, static_left, static_right = call(
        functools.partial(static_pack_kernel, steps, halo),
        [((2 * steps + 2, high, cols), F32)] + packed,
        [place, maps, courant, land_mask, below, above],
        smem=1,
        name="static_pack",
    )
    inc, to_left, to_right, early = call(
        functools.partial(pack_kernel, steps, halo, scale),
        [((3, high, cols), F32)] + packed + [((8, cols), F32)],
        [place, share, share_other, static_std, control, early, below, above, static_left, static_right],
        smem=1,
        name="pack",
    )
    from_left = lax.ppermute(to_right, "tx", right)
    from_right = lax.ppermute(to_left, "tx", left)

    (rows_ahead,) = call(
        functools.partial(ahead_kernel, ahead),
        [((own, 3, len(ahead) * UNIT, cols), BF16)],
        [perturbations, early],
        name="ahead",
    )
    ahead_others = to_others(rows_ahead, groups)

    control_new, cost_terms, lam = call(
        functools.partial(model_kernel, steps, halo),
        [((3, rows, cols), F32), ((n_ty * n_tx, cols), F32), ((3, rows, cols), F32)],
        [place, tall, inc, from_right, from_left, early, static_std, control],
        scratch=model_scratch(steps, halo, rows, cols, n_ty * n_tx),
        out_specs=[VMEM, HBM, VMEM],
        smem=1,
        mib=16,
        name="model",
    )
    sent, *products_ahead = call(
        functools.partial(products_kernel, behind, ahead),
        [((own, len(behind) * UNIT, cols), BF16)] + [((own, len(ahead) * UNIT, cols), BF16)] * groups,
        [lam, perturbations, *ahead_others],
        name="products",
    )
    sent_others = to_others(sent, groups)
    terms = lax.all_to_all(cost_terms, ("ty", "tx"), 0, 0, tiled=True)
    cost_scale = 0.5 / ((3 + members) * rows * cols * n_ty * n_tx)
    weights_new, cost = call(
        functools.partial(final_kernel, groups, scale, cost_scale, behind, ahead),
        [((own, rows, cols), F32), ((1, 1), F32)],
        [sent, *sent_others, *products_ahead, kron_grad, ens_weights, terms],
        out_specs=[VMEM, SMEM],
        name="final",
    )
    return (control_new, weights_new, cost.reshape(()))


def solution(mesh):
    return jax.shard_map(
        body,
        mesh=mesh,
        in_specs=(
            P("ens", None, "ty", "tx"),
            P("ens", "ty", "tx"),
            P(None, "ty", "tx"),
            P(None, "ty", "tx"),
            P("ty", "tx"),
            P("ty", "tx"),
            P(),
            P(),
            P("ty", "tx", None, None),
            P("ty", "tx", None, None),
            P("ty", "tx", None, None),
        ),
        out_specs=(P(None, "ty", "tx"), P("ens", "ty", "tx"), P()),
        check_vma=False,
    )
```

```python
import functools
import math

import jax
import jax.numpy as jnp
from jax import lax
from jax.experimental import pallas as pl
from jax.experimental.pallas import tpu as pltpu
from jax.sharding import PartitionSpec as P

step_length = 0.25
SUB = 16
UNIT = 2 * SUB
PIECES = 3
ROW = 8
GROUP = 24
F32 = jnp.float32
BF16 = jnp.bfloat16
VMEM = pl.BlockSpec(memory_space=pltpu.VMEM)
SMEM = pl.BlockSpec(memory_space=pltpu.SMEM)
HBM = pl.BlockSpec(memory_space=pltpu.HBM)


def call(kernel, outs, ins, scratch=(), smem=0, flops=0, name=None, mib=4, out_specs=None, in_specs=None, grid=()):
    out_shape = [jax.ShapeDtypeStruct(s, d) for s, d in outs]
    moved = sum(math.prod(s) * jnp.dtype(d).itemsize for s, d in outs)
    moved += sum(x.size * x.dtype.itemsize for x in ins)
    return pl.pallas_call(
        kernel,
        out_shape=out_shape,
        grid=grid,
        in_specs=in_specs or [SMEM] * smem + [VMEM] * (len(ins) - smem),
        out_specs=out_specs or [VMEM] * len(outs),
        scratch_shapes=list(scratch),
        compiler_params=pltpu.CompilerParams(vmem_limit_bytes=mib * 1024 * 1024),
        cost_estimate=pl.CostEstimate(flops=flops, bytes_accessed=moved, transcendentals=0),
        name=name,
    )(*ins)


def split(x):
    hi = x.astype(BF16)
    return hi, (x - hi.astype(F32)).astype(BF16)


def folded(x):
    cols = x.shape[-1]
    return jnp.sum(x.reshape(-1, 8, cols), axis=0)


def maps_kernel(steps, cells_ref, values_ref, weights_ref, control_ref, maps_ref, cost_ref):
    rows, cols = maps_ref.shape[1:]
    count = cells_ref.shape[1]
    shift = cols.bit_length() - 1
    row_iota = lax.broadcasted_iota(jnp.int32, (rows, count), 0)
    col_iota = lax.broadcasted_iota(jnp.int32, (cols, count), 0)
    for t in range(steps):
        cells = cells_ref[t : t + 1, :]
        weight = weights_ref[t : t + 1, :]
        product = weight * values_ref[t : t + 1, :]
        at_row = jnp.where(row_iota == (cells >> shift), 1.0, 0.0).astype(BF16)
        hit = col_iota == (cells & (cols - 1))
        parts = []
        for value in (weight, product):
            for piece in split(value):
                parts.append(jnp.where(hit, piece.astype(F32), 0.0).astype(BF16))
        sums = lax.dot_general(
            at_row,
            jnp.concatenate(parts, axis=0),
            (((1,), (1,)), ((), ())),
            preferred_element_type=F32,
        )
        maps_ref[t] = sums[:, :cols] + sums[:, cols : 2 * cols]
        maps_ref[steps + t] = sums[:, 2 * cols : 3 * cols] + sums[:, 3 * cols :]
    value = values_ref[...]
    fixed = jnp.sum(weights_ref[...] * value * value, axis=0, keepdims=True)
    line = sum(fixed[:, k : k + cols] for k in range(0, count, cols))
    first = lax.broadcasted_iota(jnp.int32, (8, cols), 0) == 0
    control = control_ref[...]
    cost_ref[...] = folded(control * control) + jnp.where(first, line, 0.0)


def send_kernel(chunk, alpha_ref, *refs):
    out_ref, rows_ref, sems = refs[-3:]
    copies = []
    for n, y in enumerate(chunk):
        at = slice(n * UNIT, (n + 1) * UNIT)
        copies.append(pltpu.make_async_copy(alpha_ref.at[:, y : y + UNIT, :], rows_ref.at[:, at, :], sems.at[n]))
        copies[-1].start()
    for n, copy in enumerate(copies):
        at = slice(n * UNIT, (n + 1) * UNIT)
        copy.wait()
        out_ref[:, at, :] = rows_ref[:, at, :].astype(BF16)


def expand(small):
    rows, cols = small.shape
    left = lax.broadcasted_iota(jnp.int32, (rows * SUB, rows), 0) // SUB
    left = (left == lax.broadcasted_iota(jnp.int32, (rows * SUB, rows), 1)).astype(F32).astype(BF16)
    right = lax.broadcasted_iota(jnp.int32, (cols, cols * SUB), 1) // SUB
    right = (right == lax.broadcasted_iota(jnp.int32, (cols, cols * SUB), 0)).astype(F32).astype(BF16)
    wide = jnp.dot(small, right, preferred_element_type=F32).astype(BF16)
    full = jnp.dot(left, wide, preferred_element_type=F32)
    row = lax.broadcasted_iota(jnp.int32, full.shape, 0) % SUB
    col = lax.broadcasted_iota(jnp.int32, full.shape, 1) % SUB
    return jnp.where(row == col, full, 0.0).astype(BF16)


def coefficients(own, members, axis, first_row, first_col, offsets_ref, weights_ref):
    shape = (own, own)
    row_place = lax.broadcasted_iota(jnp.int32, shape, axis)
    column = first_col + lax.broadcasted_iota(jnp.int32, shape, 1 - axis)
    shift = jnp.zeros(shape, jnp.int32)
    for j in range(own):
        shift = jnp.where(row_place == j, offsets_ref[first_row + j], shift)
    place = column - shift
    place = jnp.where(place < 0, place + members, place)
    value = jnp.zeros(shape, F32)
    for k in range(members):
        value = jnp.where(place == k, weights_ref[k], value)
    return value.astype(BF16)


def pair_of(ref, y):
    members, _, cols = ref.shape
    blocks = [ref[:, y + k * SUB : y + (k + 1) * SUB, :].reshape(members * SUB, cols) for k in (0, 1)]
    return jnp.concatenate(blocks, axis=1)


def shares(beta, perturbations_ref, y):
    members = perturbations_ref.shape[0]
    cols = perturbations_ref.shape[3]
    for k in (0, 1):
        part = beta[:, k * cols : (k + 1) * cols].reshape(members, SUB, cols)
        at = y + k * SUB
        for c in range(3):
            total = part[0] * perturbations_ref[0, c, at : at + SUB, :].astype(F32)
            for i in range(1, members):
                total = total + part[i] * perturbations_ref[i, c, at : at + SUB, :].astype(F32)
            yield k * SUB, c, total


def own_kernel(
    groups,
    place_ref,
    offsets_ref,
    weights_ref,
    alpha_hbm_ref,
    perturbations_ref,
    kron_beta_ref,
    kron_grad_ref,
    share_ref,
    square_ref,
    alpha_ref,
    sem,
):
    own, rows, cols = alpha_ref.shape
    load = pltpu.make_async_copy(alpha_hbm_ref, alpha_ref, sem)
    load.start()
    members = own * groups
    first = place_ref[2] * own
    for g in range(groups):
        other = lax.rem(place_ref[2] + g, groups) * own
        kron_beta_ref[g] = expand(coefficients(own, members, 1, other, first, offsets_ref, weights_ref))
        kron_grad_ref[g] = expand(coefficients(own, members, 0, first, other, offsets_ref, weights_ref))
    load.wait()
    matrix = kron_beta_ref[0]
    square = jnp.zeros((8, cols), F32)
    for y in range(0, rows, UNIT):
        alpha = pair_of(alpha_ref, y)
        square = square + folded(alpha[:, :cols] * alpha[:, :cols]) + folded(alpha[:, cols:] * alpha[:, cols:])
        hi, lo = split(alpha)
        beta = jnp.dot(matrix, hi, preferred_element_type=F32) + jnp.dot(matrix, lo, preferred_element_type=F32)
        for at, c, total in shares(beta, perturbations_ref, y):
            share_ref[c, y + at : y + at + SUB, :] = total
    rest = jnp.sum(square, axis=0, keepdims=True)
    pieces = []
    for _ in range(PIECES):
        pieces.append(rest.astype(BF16).astype(F32))
        rest = rest - pieces[-1]
    pieces.append(jnp.zeros((SUB - PIECES, cols), F32))
    square_ref[...] = jnp.concatenate(pieces, axis=0).astype(BF16)


def share_kernel(groups, units, *refs):
    others = refs[: groups - 1]
    kron_ref, perturbations_ref, own_ref, out_ref = refs[groups - 1 :]
    height = len(units) * UNIT
    for n, y in enumerate(units):
        beta = None
        for g, other in enumerate(others):
            term = jnp.dot(kron_ref[g + 1], pair_of(other, n * UNIT), preferred_element_type=F32)
            beta = term if beta is None else beta + term
        for at, c, total in shares(beta, perturbations_ref, y):
            total = total + own_ref[c, y + at : y + at + SUB, :]
            to = c * height + n * UNIT + at
            out_ref[to : to + SUB, :] = total.astype(BF16)


def row_sizes(steps, halo):
    reach = [-(-2 * (t + 1) // 8) * 8 for t in range(steps)]
    return reach * 2 + [halo] * 8


def whole(rows):
    return -(-rows // SUB) * SUB


def strips_kernel(steps, halo, units, share_ref, std_ref, control_ref, maps_ref, courant_ref, mask_ref, top_ref, bottom_ref):
    rows, cols = courant_ref.shape
    height = len(units) * UNIT
    share = share_ref[...].astype(F32)
    sizes = row_sizes(steps, halo)
    for ref, low, share_low in ((top_ref, True, 0), (bottom_ref, False, height - halo)):

        def pick(size):
            return slice(0, size) if low else slice(rows - size, rows)

        fields = [maps_ref[k, pick(sizes[k]), :] for k in range(2 * steps)]
        fields += [courant_ref[pick(halo), :], mask_ref[pick(halo), :].astype(F32)]
        fields += [std_ref[c, pick(halo), :] * control_ref[c, pick(halo), :] for c in range(3)]
        fields += [share[c * height + share_low : c * height + share_low + halo] for c in range(3)]
        fill = ref.shape[0] - sum(sizes)
        if fill:
            fields.append(jnp.zeros((fill, cols), F32))
        ref[...] = jnp.concatenate(fields, axis=0).astype(BF16)


def lane_pack(fields, widths, at=0, left=None, right=None):
    cols = fields[0].shape[1]
    lane = lax.broadcasted_iota(jnp.int32, fields[0].shape, 1)
    for field, width in zip(fields, widths):
        to_left = field if at == 0 else pltpu.roll(field, at, 1)
        to_right = field if at == 0 else pltpu.roll(field, cols - at, 1)
        left = to_left if left is None else jnp.where(lane >= at, to_left, left)
        right = to_right if right is None else jnp.where(lane < cols - at, to_right, right)
        at += width
    return left, right


def lane_unpack(from_right, from_left, at, width):
    cols = from_right.shape[1]
    lane = lax.broadcasted_iota(jnp.int32, from_right.shape, 1)
    if at:
        from_right = pltpu.roll(from_right, cols - at, 1)
        from_left = pltpu.roll(from_left, at, 1)
    return jnp.where(lane < width, from_right, jnp.where(lane >= cols - width, from_left, 0.0))


def lane_blocks(steps, halo):
    maps = [[(part * steps + t, 2 * (t + 1)) for t in range(steps)] for part in (0, 1)]
    at = 2 * steps
    return [maps[0] + [(at + 2 + c, halo) for c in range(3)], maps[1] + [(at, halo), (at + 1, halo)]]


def packed_blocks(steps, halo, field, left_ref, right_ref, first, place):
    for n, block in enumerate(lane_blocks(steps, halo)):
        left, right = lane_pack([field(k) for k, _ in block], [w for _, w in block])
        at = slice(n * first + place, n * first + place + left.shape[0])
        left_ref[at, :] = left.astype(BF16)
        right_ref[at, :] = right.astype(BF16)


def static_tile(steps, maps_ref, courant_ref, mask_ref, std_ref, control_ref):
    def field(k):
        if k < 2 * steps:
            return maps_ref[k]
        if k == 2 * steps:
            return courant_ref[...]
        if k == 2 * steps + 1:
            return mask_ref[...].astype(F32)
        return std_ref[k - 2 * steps - 2] * control_ref[k - 2 * steps - 2]

    return field


def tile_pack_kernel(steps, halo, maps_ref, courant_ref, mask_ref, std_ref, control_ref, left_ref, right_ref):
    field = static_tile(steps, maps_ref, courant_ref, mask_ref, std_ref, control_ref)
    packed_blocks(steps, halo, field, left_ref, right_ref, courant_ref.shape[0], 0)


def beside_rows(steps, halo, place_ref, below_ref, above_ref):
    sizes = row_sizes(steps, halo)
    cols = below_ref.shape[1]
    below = jnp.where(place_ref[1] == 1, 0.0, below_ref[...].astype(F32))
    above = jnp.where(place_ref[0] == 1, 0.0, above_ref[...].astype(F32))

    def field(k):
        at, size = sum(sizes[:k]), sizes[k]
        parts = [below[at : at + size], above[at : at + size]]
        if size < halo:
            parts.insert(1, jnp.zeros((2 * (halo - size), cols), F32))
        return jnp.concatenate(parts, axis=0)

    return field


def merge_kernel(
    steps,
    halo,
    outer,
    inner,
    place_ref,
    outer_ref,
    inner_ref,
    below_ref,
    above_ref,
    square_ref,
    tile_left_ref,
    tile_right_ref,
    out_ref,
    left_ref,
    right_ref,
    part_left_ref,
    part_right_ref,
):
    rows = (len(outer) + len(inner)) * UNIT
    high = rows + 2 * halo
    for units, ref in ((outer, outer_ref), (inner, inner_ref)):
        height = len(units) * UNIT
        for c in range(3):
            for n, y in enumerate(units):
                at = c * height + n * UNIT
                out_ref[c * rows + y : c * rows + y + UNIT, :] = ref[at : at + UNIT, :]
    field = beside_rows(steps, halo, place_ref, below_ref, above_ref)
    beside = [field(2 * steps + 5 + c) for c in range(3)]
    out_ref[3 * rows : 3 * rows + 6 * halo, :] = jnp.concatenate(beside, axis=0).astype(BF16)
    out_ref[3 * rows + 6 * halo :, :] = square_ref[...]
    for ref, tile_ref in ((left_ref, tile_left_ref), (right_ref, tile_right_ref)):
        for n in (0, 1):
            ref[n * high : n * high + rows, :] = tile_ref[n * rows : (n + 1) * rows, :]
    for n, block in enumerate(lane_blocks(steps, halo)):
        left, right = lane_pack([field(k) for k, _ in block], [w for _, w in block])
        left_ref[n * high + rows : (n + 1) * high, :] = left.astype(BF16)
        right_ref[n * high + rows : (n + 1) * high, :] = right.astype(BF16)
    shares_tall = [
        jnp.concatenate([out_ref[c * rows : (c + 1) * rows, :].astype(F32), beside[c]], axis=0) for c in range(3)
    ]
    left, right = lane_pack(shares_tall, [halo] * 3)
    part_left_ref[...] = left.astype(BF16)
    part_right_ref[...] = right.astype(BF16)


def tall_kernel(
    steps, halo, place_ref, maps_ref, courant_ref, mask_ref, std_ref, control_ref, below_ref, above_ref, tall_ref
):
    rows = courant_ref.shape[0]
    tile = static_tile(steps, maps_ref, courant_ref, mask_ref, std_ref, control_ref)
    beside = beside_rows(steps, halo, place_ref, below_ref, above_ref)
    for k in range(2 * steps + 5):
        tall_ref[k, :rows, :] = tile(k)
        tall_ref[k, rows:, :] = beside(k)


def model_kernel(
    steps,
    halo,
    scale,
    place_ref,
    tall_ref,
    own_ref,
    other_ref,
    from_right_ref,
    from_left_ref,
    part_right_ref,
    part_left_ref,
    far_right_ref,
    far_left_ref,
    early_ref,
    std_ref,
    control_ref,
    control_new_ref,
    cost_out_ref,
    lam_ref,
    source_ref,
    cost_ref,
    cost_sem,
    inc_ref,
    sides_ref,
    courant_ref,
    half_wet_ref,
    half_both_ref,
    *state_refs,
):
    _, rows, cols = control_ref.shape
    height_ext = rows + 2 * halo
    fields = 2 * steps + 2
    tile, extra, total_blocks = rows // ROW, halo // ROW, height_ext // ROW
    states = state_refs[:3], state_refs[3:]
    left, right = slice(0, cols), slice(cols, 2 * cols)
    row = lax.broadcasted_iota(jnp.int32, (ROW, 2 * cols), 0)
    top, last = row == 0, row == ROW - 1
    half = [jnp.where(place_ref[k] == 1, 0.0, 0.5) for k in (0, 1)]

    def at(k):
        k = k % total_blocks
        return slice(k * ROW, (k + 1) * ROW)

    def half_inside(k):
        return half[0] if k < 0 else half[1] if k >= tile else 0.5

    def around(reach):
        n = min(extra, -(-reach // ROW))
        return range(-n, tile + n)

    def east(x):
        return pltpu.roll(x, 2 * cols - 1, 1) - pltpu.roll(x, 1, 1)

    class Column:
        def __init__(self):
            self.value, self.up, self.down = {}, {}, {}

        def put(self, k, x):
            self.value[k], self.up[k], self.down[k] = x, pltpu.roll(x, ROW - 1, 0), pltpu.roll(x, 1, 0)

        def north(self, k):
            up = jnp.where(last, self.up.get(k + 1, self.up[k]), self.up[k])
            return up - jnp.where(top, self.down.get(k - 1, self.down[k]), self.down[k])

    part_right = part_right_ref[...].astype(F32) + far_right_ref[...].astype(F32)
    part_left = part_left_ref[...].astype(F32) + far_left_ref[...].astype(F32)
    for c in range(3):
        here = slice(c * rows, (c + 1) * rows)
        total = own_ref[here, :].astype(F32) + other_ref[here, :].astype(F32)
        inc_ref[c, :rows, :] = tall_ref[fields + c, :rows, :] + scale * total
    here = slice(3 * rows, 3 * rows + 6 * halo)
    total = own_ref[here, :].astype(F32) + other_ref[here, :].astype(F32)
    for c in range(3):
        beside = total[2 * c * halo : 2 * (c + 1) * halo]
        inc_ref[c, rows:, :] = tall_ref[fields + c, rows:, :] + scale * beside
    here = slice(3 * rows + 6 * halo, 3 * rows + 6 * halo + SUB)
    squares = own_ref[here, :].astype(F32) + other_ref[here, :].astype(F32)
    for n, block in enumerate(lane_blocks(steps, halo)):
        place = 0
        from_right = from_right_ref[n * height_ext : (n + 1) * height_ext, :].astype(F32)
        from_left = from_left_ref[n * height_ext : (n + 1) * height_ext, :].astype(F32)
        for k, size in block:
            side = lane_unpack(from_right, from_left, place, size)
            if k >= fields:
                side = side + scale * lane_unpack(part_right, part_left, (k - fields) * halo, halo)
            sides_ref[k] = side
            place += size

    def joined(k, rows_at):
        main = tall_ref[k, rows_at, :] if k < fields else inc_ref[k - fields, rows_at, :]
        return jnp.concatenate([main, sides_ref[k, rows_at, :]], axis=1)

    for k in around(halo):
        wet, courant = joined(2 * steps + 1, at(k)), joined(2 * steps, at(k))
        half_wet_ref[at(k), :] = 0.5 * wet
        courant_ref[at(k), :] = courant
        half_both_ref[at(k), :] = 0.5 * wet * courant
        states[0][0][at(k), :] = joined(fields, at(k))
        states[0][1][at(k), :] = wet * joined(fields + 1, at(k))
        states[0][2][at(k), :] = wet * joined(fields + 2, at(k))

    total = early_ref[...] + squares[:8]
    for t in range(steps):
        out = halo - 2 * (t + 1)
        src, dst = states[t % 2], states[1 - t % 2]
        flow, result, seen = around(out + 1), around(out), around(2 * (t + 1))
        height, flux, spread = Column(), Column(), {}
        for k in (flow[0] - 1, flow[0]):
            if k >= -extra:
                height.put(k, src[0][at(k), :])
        for first in range(flow[0], flow[-1] + 2, GROUP):
            group = [k for k in range(first, first + GROUP) if k in flow]
            for k in group:
                if k + 1 < tile + extra:
                    height.put(k + 1, src[0][at(k + 1), :])
            slopes = [(east(height.value[k]), height.north(k)) for k in group]
            moved = []
            for k, (x, y) in zip(group, slopes):
                half_wet = half_wet_ref[at(k), :]
                moved.append((src[1][at(k), :] - half_wet * x, src[2][at(k), :] - half_wet * y))
            for k, (u, v) in zip(group, moved):
                dst[1][at(k), :] = u
                dst[2][at(k), :] = v
            flows = []
            for k, (u, v) in zip(group, moved):
                courant = courant_ref[at(k), :]
                flows.append((courant * u, courant * v))
            for k, (u, v) in zip(group, flows):
                spread[k] = east(u)
                flux.put(k, v)
            ready = [k for k in range(first - 1, first + GROUP - 1) if k in result]
            new = [height.value[k] - half_inside(k) * (spread[k] + flux.north(k)) for k in ready]
            for k, x in zip(ready, new):
                dst[0][at(k), :] = x
            for k, x in zip(ready, new):
                if k in seen:
                    offset = joined(steps + t, at(k))
                    source = joined(t, at(k)) * x - offset
                    source_ref[t, at(k), :] = source
                    if 0 <= k < tile:
                        total = total + x[:, left] * (source[:, left] - offset[:, left])
    cost_ref[...] = jnp.broadcast_to(jnp.sum(total, axis=0, keepdims=True), cost_ref.shape)
    cost_copy = pltpu.make_async_copy(cost_ref, cost_out_ref, cost_sem)
    cost_copy.start()

    for t in range(steps - 1, -1, -1):
        given, flow, result = around(2 * (t + 1)), around(2 * t + 1), around(2 * t)
        src, dst = states[t % 2], states[1 - t % 2]
        adj, flux, spread, east_flow = Column(), Column(), {}, {}

        def load(k):
            x = source_ref[t, at(k), :]
            adj.put(k, x if t == steps - 1 else x + src[0][at(k), :])

        for k in (flow[0] - 1, flow[0]):
            if k in given:
                load(k)
        for first in range(flow[0], flow[-1] + 2, GROUP):
            group = [k for k in range(first, first + GROUP) if k in flow]
            for k in group:
                if k + 1 in given:
                    load(k + 1)
            slopes = [(east(adj.value[k]), adj.north(k)) for k in group]
            moved = []
            for k, (x, y) in zip(group, slopes):
                half_both = half_both_ref[at(k), :]
                u, v = half_both * x, half_both * y
                if t < steps - 1:
                    u = u + src[1][at(k), :]
                    v = v + src[2][at(k), :]
                moved.append((u, v))
            for k, (u, v) in zip(group, moved):
                spread[k] = east(u)
                flux.put(k, v)
            for k, (u, v) in zip(group, moved):
                if t:
                    dst[1][at(k), :] = u
                    dst[2][at(k), :] = v
                elif 0 <= k < tile:
                    lam_ref[1, at(k), :] = u[:, left]
                    lam_ref[2, at(k), :] = v[:, left]
            ready = [k for k in range(first - 1, first + GROUP - 1) if k in result]
            new = [adj.value[k] + half_inside(k) * (spread[k] + flux.north(k)) for k in ready]
            for k, x in zip(ready, new):
                if t:
                    dst[0][at(k), :] = x
                else:
                    lam_ref[0, at(k), :] = x[:, left]
    for c in range(3):
        old = control_ref[c]
        control_new_ref[c] = old - step_length * (old + std_ref[c] * lam_ref[c])
    cost_copy.wait()


def model_scratch(steps, halo, rows, cols, terms):
    high = rows + 2 * halo
    return [
        pltpu.VMEM((steps, high, 2 * cols), F32),
        pltpu.VMEM((terms, cols), F32),
        pltpu.SemaphoreType.DMA,
        pltpu.VMEM((3, high, cols), F32),
        pltpu.VMEM((2 * steps + 5, high, cols), F32),
    ] + [pltpu.VMEM((high, 2 * cols), F32)] * 9


def ahead_kernel(ahead, perturbations_ref, early_ref, out_ref):
    for n, y in enumerate(ahead):
        out_ref[:, :, n * UNIT : (n + 1) * UNIT, :] = perturbations_ref[:, :, y : y + UNIT, :]


def products_kernel(units, ahead, lam_ref, perturbations_ref, *refs):
    count = 0
    others, sent_ref, ahead_refs = refs[:count], refs[count], refs[count + 1 :]

    def products(ref, i, at, rows):
        total = ref[i, 0, at, :].astype(F32) * lam_ref[0, rows, :]
        for c in (1, 2):
            total = total + ref[i, c, at, :].astype(F32) * lam_ref[c, rows, :]
        return total.astype(BF16)

    for i in range(perturbations_ref.shape[0]):
        for n, y in enumerate(units):
            rows = slice(y, y + UNIT)
            sent_ref[i, n * UNIT : (n + 1) * UNIT, :] = products(perturbations_ref, i, rows, rows)
        for n, y in enumerate(ahead):
            rows, at = slice(y, y + UNIT), slice(n * UNIT, (n + 1) * UNIT)
            ahead_refs[0][i, at, :] = products(perturbations_ref, i, rows, rows)
            for ref, out_ref in zip(others, ahead_refs[1:]):
                out_ref[i, at, :] = products(ref, i, at, rows)


def final_kernel(groups, scale, cost_scale, units, ahead, *refs):
    late, early = refs[:groups], ()
    kron_ref, alpha_ref, terms_ref, out_ref, cost_ref = refs[groups:]
    members, rows, cols = alpha_ref.shape
    cost_ref[0, 0] = jnp.sum(terms_ref[...]) * cost_scale
    for parts, chunk in ((early, ahead), (late, units)):
        for n, y in enumerate(chunk):
            grad = None
            for g, part in enumerate(parts):
                term = jnp.dot(kron_ref[g], pair_of(part, n * UNIT), preferred_element_type=F32)
                grad = term if grad is None else grad + term
            for k in (0, 1):
                at = slice(y + k * SUB, y + (k + 1) * SUB)
                part = grad[:, k * cols : (k + 1) * cols].reshape(members, SUB, cols)
                old = alpha_ref[:, at, :]
                out_ref[:, at, :] = old - step_length * (old + scale * part)


def to_others(x, groups):
    return [lax.ppermute(x, "ens", [(i, (i - k) % groups) for i in range(groups)]) for k in range(1, groups)]


def sum_parts(share, groups):
    if groups == 2:
        return share, to_others(share, groups)[0]
    share = lax.psum(share.astype(F32), "ens")
    return share, jnp.zeros_like(share)


def body(
    perturbations,
    ens_weights,
    control,
    static_std,
    courant,
    land_mask,
    band_offsets,
    band_weights,
    obs_cells,
    obs_values,
    obs_weights,
):
    own, _, rows, cols = perturbations.shape
    groups = lax.axis_size("ens")
    n_ty, n_tx = lax.axis_size("ty"), lax.axis_size("tx")
    members = own * groups
    steps = obs_cells.shape[2]
    halo = 4 * steps
    scale = 1.0 / math.sqrt(members)
    down = [(i, (i + 1) % n_ty) for i in range(n_ty)]
    up = [(j, i) for i, j in down]
    right = [(i, (i + 1) % n_tx) for i in range(n_tx)]
    left = [(j, i) for i, j in right]
    ty_index = lax.axis_index("ty")
    place = jnp.stack(
        [
            (ty_index == 0).astype(jnp.int32),
            (ty_index == n_ty - 1).astype(jnp.int32),
            lax.axis_index("ens").astype(jnp.int32),
        ]
    )
    units = list(range(0, rows, UNIT))
    at_edge = -(-halo // UNIT)
    outer = units[:at_edge] + units[len(units) - at_edge :]
    inner = units[at_edge : len(units) - at_edge]
    ahead = []
    behind = [y for y in units if y not in ahead]

    def rows_of(chunk, mib, *before):
        shape = (own, len(chunk) * UNIT, cols)
        (sent,) = call(
            functools.partial(send_kernel, chunk),
            [(shape, BF16)],
            [ens_weights, *before],
            in_specs=[HBM] * (1 + len(before)),
            scratch=[pltpu.VMEM(shape, F32), pltpu.SemaphoreType.DMA((len(chunk),))],
            name="send",
            mib=mib,
        )
        return sent

    outer_sent = rows_of(outer, 56)
    outer_others = to_others(outer_sent, groups)

    cells, values, weights = (x.reshape(steps, x.shape[-1]) for x in (obs_cells, obs_values, obs_weights))
    maps, early = call(
        functools.partial(maps_kernel, steps),
        [((2 * steps, rows, cols), F32), ((8, cols), F32)],
        [cells, values, weights, control],
        flops=2 * steps * 4 * rows * cols * cells.shape[1],
        name="maps",
    )
    wide = own * SUB
    kron_beta, kron_grad, own_share, square = call(
        functools.partial(own_kernel, groups),
        [((groups, wide, wide), BF16)] * 2 + [((3, rows, cols), F32), ((SUB, cols), BF16)],
        [place, band_offsets, band_weights, ens_weights, perturbations],
        in_specs=[SMEM, SMEM, SMEM, HBM, VMEM],
        scratch=[pltpu.VMEM((own, rows, cols), F32), pltpu.SemaphoreType.DMA],
        name="own",
    )

    inner_others = to_others(rows_of(inner, 4, square), groups)

    def share_of(units, others, name):
        (share,) = call(
            functools.partial(share_kernel, groups, units),
            [((3 * len(units) * UNIT, cols), BF16)],
            [*others, kron_beta, perturbations, own_share],
            name=name,
        )
        return share

    outer_share = share_of(outer, outer_others, "outer_share")
    edge_rows = whole(sum(row_sizes(steps, halo)))
    top, bottom = call(
        functools.partial(strips_kernel, steps, halo, outer),
        [((edge_rows, cols), BF16)] * 2,
        [outer_share, static_std, control, maps, courant, land_mask],
        name="strips",
    )
    above = lax.ppermute(bottom, "ty", down)
    below = lax.ppermute(top, "ty", up)

    inner_share = share_of(inner, inner_others, "inner_share")
    high = rows + 2 * halo
    static = [maps, courant, land_mask, static_std, control]
    tile_left, tile_right = call(
        functools.partial(tile_pack_kernel, steps, halo),
        [((2 * rows, cols), BF16)] * 2,
        static,
        name="tile_pack",
    )
    share, to_left, to_right, part_left, part_right = call(
        functools.partial(merge_kernel, steps, halo, outer, inner),
        [((3 * rows + 6 * halo + SUB, cols), BF16)] + [((2 * high, cols), BF16)] * 2 + [((high, cols), BF16)] * 2,
        [place, outer_share, inner_share, below, above, square, tile_left, tile_right],
        smem=1,
        name="merge",
    )
    share, share_other = sum_parts(share, groups)

    def across(to, part, perm):
        if groups != 2:
            part = lax.psum(part.astype(F32), "ens")
            return lax.ppermute(to, "tx", perm), lax.ppermute(part, "tx", perm), jnp.zeros_like(part)
        got = lax.ppermute(jnp.concatenate([to, part], axis=0), "tx", perm)
        far = [(e * n_tx + i, (1 - e) * n_tx + j) for e in (0, 1) for i, j in perm]
        return got[: 2 * high], got[2 * high :], lax.ppermute(part, ("ens", "tx"), far)

    from_left, near_left, far_left = across(to_right, part_right, right)
    from_right, near_right, far_right = across(to_left, part_left, left)
    (tall,) = call(
        functools.partial(tall_kernel, steps, halo),
        [((2 * steps + 5, high, cols), F32)],
        [place, *static, below, above],
        smem=1,
        name="tall",
    )
    ahead_others = []
    control_new, cost_terms, lam = call(
        functools.partial(model_kernel, steps, halo, scale),
        [((3, rows, cols), F32), ((n_ty * n_tx, cols), F32), ((3, rows, cols), F32)],
        [
            place,
            tall,
            share,
            share_other,
            from_right,
            from_left,
            near_right,
            near_left,
            far_right,
            far_left,
            early,
            static_std,
            control,
        ],
        scratch=model_scratch(steps, halo, rows, cols, n_ty * n_tx),
        out_specs=[VMEM, HBM, VMEM],
        smem=1,
        mib=16,
        name="model",
    )
    sent, *products_ahead = call(
        functools.partial(products_kernel, behind, ahead),
        [((own, len(behind) * UNIT, cols), BF16)],
        [lam, perturbations, *ahead_others],
        name="products",
    )
    sent_others = to_others(sent, groups)
    terms = lax.all_to_all(cost_terms, ("ty", "tx"), 0, 0, tiled=True)
    cost_scale = 0.5 / ((3 + members) * rows * cols * n_ty * n_tx)
    weights_new, cost = call(
        functools.partial(final_kernel, groups, scale, cost_scale, behind, ahead),
        [((own, rows, cols), F32), ((1, 1), F32)],
        [sent, *sent_others, *products_ahead, kron_grad, ens_weights, terms],
        out_specs=[VMEM, SMEM],
        name="final",
    )
    return (control_new, weights_new, cost.reshape(()))


def solution(mesh):
    return jax.shard_map(
        body,
        mesh=mesh,
        in_specs=(
            P("ens", None, "ty", "tx"),
            P("ens", "ty", "tx"),
            P(None, "ty", "tx"),
            P(None, "ty", "tx"),
            P("ty", "tx"),
            P("ty", "tx"),
            P(),
            P(),
            P("ty", "tx", None, None),
            P("ty", "tx", None, None),
            P("ty", "tx", None, None),
        ),
        out_specs=(P(None, "ty", "tx"), P("ens", "ty", "tx"), P()),
        check_vma=False,
    )
```

```python
import functools
import math

import jax
import jax.numpy as jnp
from jax import lax
from jax.experimental import pallas as pl
from jax.experimental.pallas import tpu as pltpu
from jax.sharding import PartitionSpec as P

step_length = 0.25
SUB = 16
UNIT = 2 * SUB
PIECES = 3
ROW = 8
GROUP = 24
F32 = jnp.float32
BF16 = jnp.bfloat16
VMEM = pl.BlockSpec(memory_space=pltpu.VMEM)
SMEM = pl.BlockSpec(memory_space=pltpu.SMEM)
HBM = pl.BlockSpec(memory_space=pltpu.HBM)


def call(kernel, outs, ins, scratch=(), smem=0, flops=0, name=None, mib=4, out_specs=None, in_specs=None, grid=()):
    out_shape = [jax.ShapeDtypeStruct(s, d) for s, d in outs]
    moved = sum(math.prod(s) * jnp.dtype(d).itemsize for s, d in outs)
    moved += sum(x.size * x.dtype.itemsize for x in ins)
    return pl.pallas_call(
        kernel,
        out_shape=out_shape,
        grid=grid,
        in_specs=in_specs or [SMEM] * smem + [VMEM] * (len(ins) - smem),
        out_specs=out_specs or [VMEM] * len(outs),
        scratch_shapes=list(scratch),
        compiler_params=pltpu.CompilerParams(vmem_limit_bytes=mib * 1024 * 1024),
        cost_estimate=pl.CostEstimate(flops=flops, bytes_accessed=moved, transcendentals=0),
        name=name,
    )(*ins)


def split(x):
    hi = x.astype(BF16)
    return hi, (x - hi.astype(F32)).astype(BF16)


def folded(x):
    cols = x.shape[-1]
    return jnp.sum(x.reshape(-1, 8, cols), axis=0)


def maps_kernel(steps, cells_ref, values_ref, weights_ref, control_ref, maps_ref, cost_ref):
    rows, cols = maps_ref.shape[1:]
    count = cells_ref.shape[1]
    shift = cols.bit_length() - 1
    row_iota = lax.broadcasted_iota(jnp.int32, (rows, count), 0)
    col_iota = lax.broadcasted_iota(jnp.int32, (cols, count), 0)
    for t in range(steps):
        cells = cells_ref[t : t + 1, :]
        weight = weights_ref[t : t + 1, :]
        product = weight * values_ref[t : t + 1, :]
        at_row = jnp.where(row_iota == (cells >> shift), 1.0, 0.0).astype(BF16)
        hit = col_iota == (cells & (cols - 1))
        parts = []
        for value in (weight, product):
            for piece in split(value):
                parts.append(jnp.where(hit, piece.astype(F32), 0.0).astype(BF16))
        sums = lax.dot_general(
            at_row,
            jnp.concatenate(parts, axis=0),
            (((1,), (1,)), ((), ())),
            preferred_element_type=F32,
        )
        maps_ref[t] = sums[:, :cols] + sums[:, cols : 2 * cols]
        maps_ref[steps + t] = sums[:, 2 * cols : 3 * cols] + sums[:, 3 * cols :]
    value = values_ref[...]
    fixed = jnp.sum(weights_ref[...] * value * value, axis=0, keepdims=True)
    line = sum(fixed[:, k : k + cols] for k in range(0, count, cols))
    first = lax.broadcasted_iota(jnp.int32, (8, cols), 0) == 0
    control = control_ref[...]
    cost_ref[...] = folded(control * control) + jnp.where(first, line, 0.0)


def send_kernel(chunk, alpha_ref, *refs):
    out_ref, rows_ref, sems = refs[-3:]
    copies = []
    for n, y in enumerate(chunk):
        at = slice(n * UNIT, (n + 1) * UNIT)
        copies.append(pltpu.make_async_copy(alpha_ref.at[:, y : y + UNIT, :], rows_ref.at[:, at, :], sems.at[n]))
        copies[-1].start()
    for n, copy in enumerate(copies):
        at = slice(n * UNIT, (n + 1) * UNIT)
        copy.wait()
        out_ref[:, at, :] = rows_ref[:, at, :].astype(BF16)


def expand(small):
    rows, cols = small.shape
    left = lax.broadcasted_iota(jnp.int32, (rows * SUB, rows), 0) // SUB
    left = (left == lax.broadcasted_iota(jnp.int32, (rows * SUB, rows), 1)).astype(F32).astype(BF16)
    right = lax.broadcasted_iota(jnp.int32, (cols, cols * SUB), 1) // SUB
    right = (right == lax.broadcasted_iota(jnp.int32, (cols, cols * SUB), 0)).astype(F32).astype(BF16)
    wide = jnp.dot(small, right, preferred_element_type=F32).astype(BF16)
    full = jnp.dot(left, wide, preferred_element_type=F32)
    row = lax.broadcasted_iota(jnp.int32, full.shape, 0) % SUB
    col = lax.broadcasted_iota(jnp.int32, full.shape, 1) % SUB
    return jnp.where(row == col, full, 0.0).astype(BF16)


def coefficients(own, members, axis, first_row, first_col, offsets_ref, weights_ref):
    shape = (own, own)
    row_place = lax.broadcasted_iota(jnp.int32, shape, axis)
    column = first_col + lax.broadcasted_iota(jnp.int32, shape, 1 - axis)
    shift = jnp.zeros(shape, jnp.int32)
    for j in range(own):
        shift = jnp.where(row_place == j, offsets_ref[first_row + j], shift)
    place = column - shift
    place = jnp.where(place < 0, place + members, place)
    value = jnp.zeros(shape, F32)
    for k in range(members):
        value = jnp.where(place == k, weights_ref[k], value)
    return value.astype(BF16)


def pair_of(ref, y):
    members, _, cols = ref.shape
    blocks = [ref[:, y + k * SUB : y + (k + 1) * SUB, :].reshape(members * SUB, cols) for k in (0, 1)]
    return jnp.concatenate(blocks, axis=1)


def shares(beta, perturbations_ref, y):
    members = perturbations_ref.shape[0]
    cols = perturbations_ref.shape[3]
    for k in (0, 1):
        part = beta[:, k * cols : (k + 1) * cols].reshape(members, SUB, cols)
        at = y + k * SUB
        for c in range(3):
            total = part[0] * perturbations_ref[0, c, at : at + SUB, :].astype(F32)
            for i in range(1, members):
                total = total + part[i] * perturbations_ref[i, c, at : at + SUB, :].astype(F32)
            yield k * SUB, c, total


def own_kernel(
    groups,
    place_ref,
    offsets_ref,
    weights_ref,
    alpha_hbm_ref,
    perturbations_ref,
    kron_beta_ref,
    kron_grad_ref,
    share_ref,
    square_ref,
    alpha_ref,
    sem,
):
    own, rows, cols = alpha_ref.shape
    load = pltpu.make_async_copy(alpha_hbm_ref, alpha_ref, sem)
    load.start()
    members = own * groups
    first = place_ref[2] * own
    for g in range(groups):
        other = lax.rem(place_ref[2] + g, groups) * own
        kron_beta_ref[g] = expand(coefficients(own, members, 1, other, first, offsets_ref, weights_ref))
        kron_grad_ref[g] = expand(coefficients(own, members, 0, first, other, offsets_ref, weights_ref))
    load.wait()
    matrix = kron_beta_ref[0]
    square = jnp.zeros((8, cols), F32)
    for y in range(0, rows, UNIT):
        alpha = pair_of(alpha_ref, y)
        square = square + folded(alpha[:, :cols] * alpha[:, :cols]) + folded(alpha[:, cols:] * alpha[:, cols:])
        hi, lo = split(alpha)
        beta = jnp.dot(matrix, hi, preferred_element_type=F32) + jnp.dot(matrix, lo, preferred_element_type=F32)
        for at, c, total in shares(beta, perturbations_ref, y):
            share_ref[c, y + at : y + at + SUB, :] = total
    rest = jnp.sum(square, axis=0, keepdims=True)
    pieces = []
    for _ in range(PIECES):
        pieces.append(rest.astype(BF16).astype(F32))
        rest = rest - pieces[-1]
    pieces.append(jnp.zeros((SUB - PIECES, cols), F32))
    square_ref[...] = jnp.concatenate(pieces, axis=0).astype(BF16)


def share_kernel(groups, units, *refs):
    others = refs[: groups - 1]
    kron_ref, perturbations_ref, own_ref, out_ref = refs[groups - 1 :]
    height = len(units) * UNIT
    for n, y in enumerate(units):
        beta = None
        for g, other in enumerate(others):
            term = jnp.dot(kron_ref[g + 1], pair_of(other, n * UNIT), preferred_element_type=F32)
            beta = term if beta is None else beta + term
        for at, c, total in shares(beta, perturbations_ref, y):
            total = total + own_ref[c, y + at : y + at + SUB, :]
            to = c * height + n * UNIT + at
            out_ref[to : to + SUB, :] = total.astype(BF16)


def row_sizes(steps, halo):
    reach = [-(-2 * (t + 1) // 8) * 8 for t in range(steps)]
    return reach * 2 + [halo] * 8


def whole(rows):
    return -(-rows // SUB) * SUB


def strips_kernel(steps, halo, units, share_ref, std_ref, control_ref, maps_ref, courant_ref, mask_ref, top_ref, bottom_ref):
    rows, cols = courant_ref.shape
    height = len(units) * UNIT
    share = share_ref[...].astype(F32)
    sizes = row_sizes(steps, halo)
    for ref, low, share_low in ((top_ref, True, 0), (bottom_ref, False, height - halo)):

        def pick(size):
            return slice(0, size) if low else slice(rows - size, rows)

        fields = [maps_ref[k, pick(sizes[k]), :] for k in range(2 * steps)]
        fields += [courant_ref[pick(halo), :], mask_ref[pick(halo), :].astype(F32)]
        fields += [std_ref[c, pick(halo), :] * control_ref[c, pick(halo), :] for c in range(3)]
        fields += [share[c * height + share_low : c * height + share_low + halo] for c in range(3)]
        fill = ref.shape[0] - sum(sizes)
        if fill:
            fields.append(jnp.zeros((fill, cols), F32))
        ref[...] = jnp.concatenate(fields, axis=0).astype(BF16)


def lane_pack(fields, widths, at=0, left=None, right=None):
    cols = fields[0].shape[1]
    lane = lax.broadcasted_iota(jnp.int32, fields[0].shape, 1)
    for field, width in zip(fields, widths):
        to_left = field if at == 0 else pltpu.roll(field, at, 1)
        to_right = field if at == 0 else pltpu.roll(field, cols - at, 1)
        left = to_left if left is None else jnp.where(lane >= at, to_left, left)
        right = to_right if right is None else jnp.where(lane < cols - at, to_right, right)
        at += width
    return left, right


def lane_unpack(from_right, from_left, at, width):
    cols = from_right.shape[1]
    lane = lax.broadcasted_iota(jnp.int32, from_right.shape, 1)
    if at:
        from_right = pltpu.roll(from_right, cols - at, 1)
        from_left = pltpu.roll(from_left, at, 1)
    return jnp.where(lane < width, from_right, jnp.where(lane >= cols - width, from_left, 0.0))


def lane_blocks(steps, halo):
    maps = [[(part * steps + t, 2 * (t + 1)) for t in range(steps)] for part in (0, 1)]
    at = 2 * steps
    return [maps[0] + [(at + 2 + c, halo) for c in range(3)], maps[1] + [(at, halo), (at + 1, halo)]]


def packed_blocks(steps, halo, field, left_ref, right_ref, first, place):
    for n, block in enumerate(lane_blocks(steps, halo)):
        left, right = lane_pack([field(k) for k, _ in block], [w for _, w in block])
        at = slice(n * first + place, n * first + place + left.shape[0])
        left_ref[at, :] = left.astype(BF16)
        right_ref[at, :] = right.astype(BF16)


def static_tile(steps, maps_ref, courant_ref, mask_ref, std_ref, control_ref):
    def field(k):
        if k < 2 * steps:
            return maps_ref[k]
        if k == 2 * steps:
            return courant_ref[...]
        if k == 2 * steps + 1:
            return mask_ref[...].astype(F32)
        return std_ref[k - 2 * steps - 2] * control_ref[k - 2 * steps - 2]

    return field


def tile_pack_kernel(steps, halo, maps_ref, courant_ref, mask_ref, std_ref, control_ref, left_ref, right_ref):
    field = static_tile(steps, maps_ref, courant_ref, mask_ref, std_ref, control_ref)
    packed_blocks(steps, halo, field, left_ref, right_ref, courant_ref.shape[0], 0)


def beside_rows(steps, halo, place_ref, below_ref, above_ref):
    sizes = row_sizes(steps, halo)
    cols = below_ref.shape[1]
    below = jnp.where(place_ref[1] == 1, 0.0, below_ref[...].astype(F32))
    above = jnp.where(place_ref[0] == 1, 0.0, above_ref[...].astype(F32))

    def field(k):
        at, size = sum(sizes[:k]), sizes[k]
        parts = [below[at : at + size], above[at : at + size]]
        if size < halo:
            parts.insert(1, jnp.zeros((2 * (halo - size), cols), F32))
        return jnp.concatenate(parts, axis=0)

    return field


def merge_kernel(
    steps,
    halo,
    outer,
    inner,
    place_ref,
    outer_ref,
    inner_ref,
    below_ref,
    above_ref,
    square_ref,
    tile_left_ref,
    tile_right_ref,
    out_ref,
    left_ref,
    right_ref,
    part_left_ref,
    part_right_ref,
):
    rows = (len(outer) + len(inner)) * UNIT
    high = rows + 2 * halo
    for units, ref in ((outer, outer_ref), (inner, inner_ref)):
        height = len(units) * UNIT
        for c in range(3):
            for n, y in enumerate(units):
                at = c * height + n * UNIT
                out_ref[c * rows + y : c * rows + y + UNIT, :] = ref[at : at + UNIT, :]
    field = beside_rows(steps, halo, place_ref, below_ref, above_ref)
    beside = [field(2 * steps + 5 + c) for c in range(3)]
    out_ref[3 * rows : 3 * rows + 6 * halo, :] = jnp.concatenate(beside, axis=0).astype(BF16)
    out_ref[3 * rows + 6 * halo :, :] = square_ref[...]
    for ref, tile_ref in ((left_ref, tile_left_ref), (right_ref, tile_right_ref)):
        for n in (0, 1):
            ref[n * high : n * high + rows, :] = tile_ref[n * rows : (n + 1) * rows, :]
    for n, block in enumerate(lane_blocks(steps, halo)):
        left, right = lane_pack([field(k) for k, _ in block], [w for _, w in block])
        left_ref[n * high + rows : (n + 1) * high, :] = left.astype(BF16)
        right_ref[n * high + rows : (n + 1) * high, :] = right.astype(BF16)
    shares_tall = [
        jnp.concatenate([out_ref[c * rows : (c + 1) * rows, :].astype(F32), beside[c]], axis=0) for c in range(3)
    ]
    left, right = lane_pack(shares_tall, [halo] * 3)
    for ref, part_ref, part in ((left_ref, part_left_ref, left), (right_ref, part_right_ref, right)):
        part_ref[...] = part.astype(BF16)
        ref[2 * high :, :] = part.astype(BF16)


def tall_kernel(
    steps, halo, place_ref, maps_ref, courant_ref, mask_ref, std_ref, control_ref, below_ref, above_ref, tall_ref
):
    rows = courant_ref.shape[0]
    tile = static_tile(steps, maps_ref, courant_ref, mask_ref, std_ref, control_ref)
    beside = beside_rows(steps, halo, place_ref, below_ref, above_ref)
    for k in range(2 * steps + 5):
        tall_ref[k, :rows, :] = tile(k)
        tall_ref[k, rows:, :] = beside(k)


def model_kernel(
    steps,
    halo,
    scale,
    place_ref,
    tall_ref,
    own_ref,
    other_ref,
    from_right_ref,
    from_left_ref,
    far_right_ref,
    far_left_ref,
    early_ref,
    std_ref,
    control_ref,
    control_new_ref,
    cost_out_ref,
    lam_ref,
    source_ref,
    cost_ref,
    cost_sem,
    inc_ref,
    sides_ref,
    courant_ref,
    half_wet_ref,
    half_both_ref,
    *state_refs,
):
    _, rows, cols = control_ref.shape
    height_ext = rows + 2 * halo
    fields = 2 * steps + 2
    tile, extra, total_blocks = rows // ROW, halo // ROW, height_ext // ROW
    states = state_refs[:3], state_refs[3:]
    left, right = slice(0, cols), slice(cols, 2 * cols)
    row = lax.broadcasted_iota(jnp.int32, (ROW, 2 * cols), 0)
    top, last = row == 0, row == ROW - 1
    half = [jnp.where(place_ref[k] == 1, 0.0, 0.5) for k in (0, 1)]

    def at(k):
        k = k % total_blocks
        return slice(k * ROW, (k + 1) * ROW)

    def half_inside(k):
        return half[0] if k < 0 else half[1] if k >= tile else 0.5

    def around(reach):
        n = min(extra, -(-reach // ROW))
        return range(-n, tile + n)

    def east(x):
        return pltpu.roll(x, 2 * cols - 1, 1) - pltpu.roll(x, 1, 1)

    class Column:
        def __init__(self):
            self.value, self.up, self.down = {}, {}, {}

        def put(self, k, x):
            self.value[k], self.up[k], self.down[k] = x, pltpu.roll(x, ROW - 1, 0), pltpu.roll(x, 1, 0)

        def north(self, k):
            up = jnp.where(last, self.up.get(k + 1, self.up[k]), self.up[k])
            return up - jnp.where(top, self.down.get(k - 1, self.down[k]), self.down[k])

    part_right = from_right_ref[2 * height_ext :, :].astype(F32) + far_right_ref[...].astype(F32)
    part_left = from_left_ref[2 * height_ext :, :].astype(F32) + far_left_ref[...].astype(F32)
    for c in range(3):
        here = slice(c * rows, (c + 1) * rows)
        total = own_ref[here, :].astype(F32) + other_ref[here, :].astype(F32)
        inc_ref[c, :rows, :] = tall_ref[fields + c, :rows, :] + scale * total
    here = slice(3 * rows, 3 * rows + 6 * halo)
    total = own_ref[here, :].astype(F32) + other_ref[here, :].astype(F32)
    for c in range(3):
        beside = total[2 * c * halo : 2 * (c + 1) * halo]
        inc_ref[c, rows:, :] = tall_ref[fields + c, rows:, :] + scale * beside
    here = slice(3 * rows + 6 * halo, 3 * rows + 6 * halo + SUB)
    squares = own_ref[here, :].astype(F32) + other_ref[here, :].astype(F32)
    for n, block in enumerate(lane_blocks(steps, halo)):
        place = 0
        from_right = from_right_ref[n * height_ext : (n + 1) * height_ext, :].astype(F32)
        from_left = from_left_ref[n * height_ext : (n + 1) * height_ext, :].astype(F32)
        for k, size in block:
            side = lane_unpack(from_right, from_left, place, size)
            if k >= fields:
                side = side + scale * lane_unpack(part_right, part_left, (k - fields) * halo, halo)
            sides_ref[k] = side
            place += size

    def joined(k, rows_at):
        main = tall_ref[k, rows_at, :] if k < fields else inc_ref[k - fields, rows_at, :]
        return jnp.concatenate([main, sides_ref[k, rows_at, :]], axis=1)

    for k in around(halo):
        wet, courant = joined(2 * steps + 1, at(k)), joined(2 * steps, at(k))
        half_wet_ref[at(k), :] = 0.5 * wet
        courant_ref[at(k), :] = courant
        half_both_ref[at(k), :] = 0.5 * wet * courant
        states[0][0][at(k), :] = joined(fields, at(k))
        states[0][1][at(k), :] = wet * joined(fields + 1, at(k))
        states[0][2][at(k), :] = wet * joined(fields + 2, at(k))

    total = early_ref[...] + squares[:8]
    for t in range(steps):
        out = halo - 2 * (t + 1)
        src, dst = states[t % 2], states[1 - t % 2]
        flow, result, seen = around(out + 1), around(out), around(2 * (t + 1))
        height, flux, spread = Column(), Column(), {}
        for k in (flow[0] - 1, flow[0]):
            if k >= -extra:
                height.put(k, src[0][at(k), :])
        for first in range(flow[0], flow[-1] + 2, GROUP):
            group = [k for k in range(first, first + GROUP) if k in flow]
            for k in group:
                if k + 1 < tile + extra:
                    height.put(k + 1, src[0][at(k + 1), :])
            slopes = [(east(height.value[k]), height.north(k)) for k in group]
            moved = []
            for k, (x, y) in zip(group, slopes):
                half_wet = half_wet_ref[at(k), :]
                moved.append((src[1][at(k), :] - half_wet * x, src[2][at(k), :] - half_wet * y))
            for k, (u, v) in zip(group, moved):
                dst[1][at(k), :] = u
                dst[2][at(k), :] = v
            flows = []
            for k, (u, v) in zip(group, moved):
                courant = courant_ref[at(k), :]
                flows.append((courant * u, courant * v))
            for k, (u, v) in zip(group, flows):
                spread[k] = east(u)
                flux.put(k, v)
            ready = [k for k in range(first - 1, first + GROUP - 1) if k in result]
            new = [height.value[k] - half_inside(k) * (spread[k] + flux.north(k)) for k in ready]
            for k, x in zip(ready, new):
                dst[0][at(k), :] = x
            for k, x in zip(ready, new):
                if k in seen:
                    offset = joined(steps + t, at(k))
                    source = joined(t, at(k)) * x - offset
                    source_ref[t, at(k), :] = source
                    if 0 <= k < tile:
                        total = total + x[:, left] * (source[:, left] - offset[:, left])
    cost_ref[...] = jnp.broadcast_to(jnp.sum(total, axis=0, keepdims=True), cost_ref.shape)
    cost_copy = pltpu.make_async_copy(cost_ref, cost_out_ref, cost_sem)
    cost_copy.start()

    for t in range(steps - 1, -1, -1):
        given, flow, result = around(2 * (t + 1)), around(2 * t + 1), around(2 * t)
        src, dst = states[t % 2], states[1 - t % 2]
        adj, flux, spread, east_flow = Column(), Column(), {}, {}

        def load(k):
            x = source_ref[t, at(k), :]
            adj.put(k, x if t == steps - 1 else x + src[0][at(k), :])

        for k in (flow[0] - 1, flow[0]):
            if k in given:
                load(k)
        for first in range(flow[0], flow[-1] + 2, GROUP):
            group = [k for k in range(first, first + GROUP) if k in flow]
            for k in group:
                if k + 1 in given:
                    load(k + 1)
            slopes = [(east(adj.value[k]), adj.north(k)) for k in group]
            moved = []
            for k, (x, y) in zip(group, slopes):
                half_both = half_both_ref[at(k), :]
                u, v = half_both * x, half_both * y
                if t < steps - 1:
                    u = u + src[1][at(k), :]
                    v = v + src[2][at(k), :]
                moved.append((u, v))
            for k, (u, v) in zip(group, moved):
                spread[k] = east(u)
                flux.put(k, v)
            for k, (u, v) in zip(group, moved):
                if t:
                    dst[1][at(k), :] = u
                    dst[2][at(k), :] = v
                elif 0 <= k < tile:
                    lam_ref[1, at(k), :] = u[:, left]
                    lam_ref[2, at(k), :] = v[:, left]
            ready = [k for k in range(first - 1, first + GROUP - 1) if k in result]
            new = [adj.value[k] + half_inside(k) * (spread[k] + flux.north(k)) for k in ready]
            for k, x in zip(ready, new):
                if t:
                    dst[0][at(k), :] = x
                else:
                    lam_ref[0, at(k), :] = x[:, left]
    for c in range(3):
        old = control_ref[c]
        control_new_ref[c] = old - step_length * (old + std_ref[c] * lam_ref[c])
    cost_copy.wait()


def model_scratch(steps, halo, rows, cols, terms):
    high = rows + 2 * halo
    return [
        pltpu.VMEM((steps, high, 2 * cols), F32),
        pltpu.VMEM((terms, cols), F32),
        pltpu.SemaphoreType.DMA,
        pltpu.VMEM((3, high, cols), F32),
        pltpu.VMEM((2 * steps + 5, high, cols), F32),
    ] + [pltpu.VMEM((high, 2 * cols), F32)] * 9


def ahead_kernel(ahead, perturbations_ref, early_ref, out_ref):
    for n, y in enumerate(ahead):
        out_ref[:, :, n * UNIT : (n + 1) * UNIT, :] = perturbations_ref[:, :, y : y + UNIT, :]


def products_kernel(units, ahead, lam_ref, perturbations_ref, *refs):
    count = 0
    others, sent_ref, ahead_refs = refs[:count], refs[count], refs[count + 1 :]

    def products(ref, i, at, rows):
        total = ref[i, 0, at, :].astype(F32) * lam_ref[0, rows, :]
        for c in (1, 2):
            total = total + ref[i, c, at, :].astype(F32) * lam_ref[c, rows, :]
        return total.astype(BF16)

    for i in range(perturbations_ref.shape[0]):
        for n, y in enumerate(units):
            rows = slice(y, y + UNIT)
            sent_ref[i, n * UNIT : (n + 1) * UNIT, :] = products(perturbations_ref, i, rows, rows)
        for n, y in enumerate(ahead):
            rows, at = slice(y, y + UNIT), slice(n * UNIT, (n + 1) * UNIT)
            ahead_refs[0][i, at, :] = products(perturbations_ref, i, rows, rows)
            for ref, out_ref in zip(others, ahead_refs[1:]):
                out_ref[i, at, :] = products(ref, i, at, rows)


def final_kernel(groups, scale, cost_scale, units, ahead, *refs):
    late, early = refs[:groups], ()
    kron_ref, alpha_ref, terms_ref, out_ref, cost_ref = refs[groups:]
    members, rows, cols = alpha_ref.shape
    cost_ref[0, 0] = jnp.sum(terms_ref[...]) * cost_scale
    for parts, chunk in ((early, ahead), (late, units)):
        for n, y in enumerate(chunk):
            grad = None
            for g, part in enumerate(parts):
                term = jnp.dot(kron_ref[g], pair_of(part, n * UNIT), preferred_element_type=F32)
                grad = term if grad is None else grad + term
            for k in (0, 1):
                at = slice(y + k * SUB, y + (k + 1) * SUB)
                part = grad[:, k * cols : (k + 1) * cols].reshape(members, SUB, cols)
                old = alpha_ref[:, at, :]
                out_ref[:, at, :] = old - step_length * (old + scale * part)


def to_others(x, groups):
    return [lax.ppermute(x, "ens", [(i, (i - k) % groups) for i in range(groups)]) for k in range(1, groups)]


def sum_parts(share, groups):
    if groups == 2:
        return share, to_others(share, groups)[0]
    share = lax.psum(share.astype(F32), "ens")
    return share, jnp.zeros_like(share)


def body(
    perturbations,
    ens_weights,
    control,
    static_std,
    courant,
    land_mask,
    band_offsets,
    band_weights,
    obs_cells,
    obs_values,
    obs_weights,
):
    own, _, rows, cols = perturbations.shape
    groups = lax.axis_size("ens")
    n_ty, n_tx = lax.axis_size("ty"), lax.axis_size("tx")
    members = own * groups
    steps = obs_cells.shape[2]
    halo = 4 * steps
    scale = 1.0 / math.sqrt(members)
    down = [(i, (i + 1) % n_ty) for i in range(n_ty)]
    up = [(j, i) for i, j in down]
    right = [(i, (i + 1) % n_tx) for i in range(n_tx)]
    left = [(j, i) for i, j in right]
    ty_index = lax.axis_index("ty")
    place = jnp.stack(
        [
            (ty_index == 0).astype(jnp.int32),
            (ty_index == n_ty - 1).astype(jnp.int32),
            lax.axis_index("ens").astype(jnp.int32),
        ]
    )
    units = list(range(0, rows, UNIT))
    at_edge = -(-halo // UNIT)
    outer = units[:at_edge] + units[len(units) - at_edge :]
    inner = units[at_edge : len(units) - at_edge]
    ahead = []
    behind = [y for y in units if y not in ahead]

    def rows_of(chunk, mib, *before):
        shape = (own, len(chunk) * UNIT, cols)
        (sent,) = call(
            functools.partial(send_kernel, chunk),
            [(shape, BF16)],
            [ens_weights, *before],
            in_specs=[HBM] * (1 + len(before)),
            scratch=[pltpu.VMEM(shape, F32), pltpu.SemaphoreType.DMA((len(chunk),))],
            name="send",
            mib=mib,
        )
        return sent

    outer_sent = rows_of(outer, 56)
    outer_others = to_others(outer_sent, groups)

    cells, values, weights = (x.reshape(steps, x.shape[-1]) for x in (obs_cells, obs_values, obs_weights))
    maps, early = call(
        functools.partial(maps_kernel, steps),
        [((2 * steps, rows, cols), F32), ((8, cols), F32)],
        [cells, values, weights, control],
        flops=2 * steps * 4 * rows * cols * cells.shape[1],
        name="maps",
    )
    wide = own * SUB
    kron_beta, kron_grad, own_share, square = call(
        functools.partial(own_kernel, groups),
        [((groups, wide, wide), BF16)] * 2 + [((3, rows, cols), F32), ((SUB, cols), BF16)],
        [place, band_offsets, band_weights, ens_weights, perturbations],
        in_specs=[SMEM, SMEM, SMEM, HBM, VMEM],
        scratch=[pltpu.VMEM((own, rows, cols), F32), pltpu.SemaphoreType.DMA],
        name="own",
    )

    inner_others = to_others(rows_of(inner, 4, square), groups)

    def share_of(units, others, name):
        (share,) = call(
            functools.partial(share_kernel, groups, units),
            [((3 * len(units) * UNIT, cols), BF16)],
            [*others, kron_beta, perturbations, own_share],
            name=name,
        )
        return share

    outer_share = share_of(outer, outer_others, "outer_share")
    edge_rows = whole(sum(row_sizes(steps, halo)))
    top, bottom = call(
        functools.partial(strips_kernel, steps, halo, outer),
        [((edge_rows, cols), BF16)] * 2,
        [outer_share, static_std, control, maps, courant, land_mask],
        name="strips",
    )
    above = lax.ppermute(bottom, "ty", down)
    below = lax.ppermute(top, "ty", up)

    inner_share = share_of(inner, inner_others, "inner_share")
    high = rows + 2 * halo
    static = [maps, courant, land_mask, static_std, control]
    tile_left, tile_right = call(
        functools.partial(tile_pack_kernel, steps, halo),
        [((2 * rows, cols), BF16)] * 2,
        static,
        name="tile_pack",
    )
    share, to_left, to_right, part_left, part_right = call(
        functools.partial(merge_kernel, steps, halo, outer, inner),
        [((3 * rows + 6 * halo + SUB, cols), BF16)] + [((3 * high, cols), BF16)] * 2 + [((high, cols), BF16)] * 2,
        [place, outer_share, inner_share, below, above, square, tile_left, tile_right],
        smem=1,
        name="merge",
    )
    share, share_other = sum_parts(share, groups)

    def across(to, part, perm):
        if groups != 2:
            part = lax.psum(part.astype(F32), "ens")
            sent = jnp.concatenate([to[: 2 * high].astype(F32), part], axis=0)
            return lax.ppermute(sent, "tx", perm), jnp.zeros_like(part)
        far = [(e * n_tx + i, (1 - e) * n_tx + j) for e in (0, 1) for i, j in perm]
        return lax.ppermute(to, "tx", perm), lax.ppermute(part, ("ens", "tx"), far)

    from_left, far_left = across(to_right, part_right, right)
    from_right, far_right = across(to_left, part_left, left)
    (tall,) = call(
        functools.partial(tall_kernel, steps, halo),
        [((2 * steps + 5, high, cols), F32)],
        [place, *static, below, above],
        smem=1,
        name="tall",
    )
    ahead_others = []
    control_new, cost_terms, lam = call(
        functools.partial(model_kernel, steps, halo, scale),
        [((3, rows, cols), F32), ((n_ty * n_tx, cols), F32), ((3, rows, cols), F32)],
        [
            place,
            tall,
            share,
            share_other,
            from_right,
            from_left,
            far_right,
            far_left,
            early,
            static_std,
            control,
        ],
        scratch=model_scratch(steps, halo, rows, cols, n_ty * n_tx),
        out_specs=[VMEM, HBM, VMEM],
        smem=1,
        mib=16,
        name="model",
    )
    sent, *products_ahead = call(
        functools.partial(products_kernel, behind, ahead),
        [((own, len(behind) * UNIT, cols), BF16)],
        [lam, perturbations, *ahead_others],
        name="products",
    )
    sent_others = to_others(sent, groups)
    terms = lax.all_to_all(cost_terms, ("ty", "tx"), 0, 0, tiled=True)
    cost_scale = 0.5 / ((3 + members) * rows * cols * n_ty * n_tx)
    weights_new, cost = call(
        functools.partial(final_kernel, groups, scale, cost_scale, behind, ahead),
        [((own, rows, cols), F32), ((1, 1), F32)],
        [sent, *sent_others, *products_ahead, kron_grad, ens_weights, terms],
        out_specs=[VMEM, SMEM],
        name="final",
    )
    return (control_new, weights_new, cost.reshape(()))


def solution(mesh):
    return jax.shard_map(
        body,
        mesh=mesh,
        in_specs=(
            P("ens", None, "ty", "tx"),
            P("ens", "ty", "tx"),
            P(None, "ty", "tx"),
            P(None, "ty", "tx"),
            P("ty", "tx"),
            P("ty", "tx"),
            P(),
            P(),
            P("ty", "tx", None, None),
            P("ty", "tx", None, None),
            P("ty", "tx", None, None),
        ),
        out_specs=(P(None, "ty", "tx"), P("ens", "ty", "tx"), P()),
        check_vma=False,
    )
```
